32 devices in a mesh: rep: 2 (over x), attn: 2 (over core), ffn: 8 (over z, y).
Axes of the slice: x: 2, y: 2, z: 4, core: 2. Of those that a mesh axis runs over, the one named last changes fastest.
Arguments:
- queries: bfloat16 [256, 2, 4096], P(('rep', 'attn', 'ffn')), parts along dimension 0, may hold values from -8 to 8
- new_keys: bfloat16 [256, 2, 512], P(('rep', 'attn', 'ffn')), parts along dimension 0, may hold values from -6 to 6
- new_values: bfloat16 [256, 2, 512], P(('rep', 'attn', 'ffn')), parts along dimension 0, may hold values from -6 to 6
- key_cache: bfloat16 [256, 256, 512], P(('rep', 'attn', 'ffn')), parts along dimension 0, may hold values from -6 to 6
- value_cache: bfloat16 [256, 256, 512], P(('rep', 'attn', 'ffn')), parts along dimension 0, may hold values from -6 to 6
- residual_in: bfloat16 [256, 2, 4096], P(('rep', 'attn', 'ffn')), parts along dimension 0, may hold values from -40 to 40
- norm_gain: bfloat16 [4096], replicated, may hold values from 0.099609375 to 1.8984375
- gate_weight: bfloat16 [4096, 14336], P(None, ('attn', 'ffn')), may hold values from -0.09375 to 0.09375
- up_weight: bfloat16 [4096, 14336], P(None, ('attn', 'ffn')), may hold values from -0.09375 to 0.09375
- down_weight: bfloat16 [14336, 4096], P(('attn', 'ffn')), may hold values from -0.046875 to 0.046875
- live_counts: int32 [32], P(('rep', 'attn', 'ffn')), parts along dimension 0, may hold values from 6 to 8, as said below
- cache_lengths: int32 [256], P(('rep', 'attn', 'ffn')), parts along dimension 0, may hold values from 2 to 256, as said below
- positions: int32 [256], P(('rep', 'attn', 'ffn')), parts along dimension 0, may hold values from 256 to 1023
Outputs:
- layer_out: bfloat16 [256, 2, 4096], P(('rep', 'attn', 'ffn')), parts along dimension 0
The draws below stay inside these ranges and needn't reach their ends.
There are 2 independent parts, one for each index of `rep`. The reference program is written for one: setup_inputs(seed, part) draws one part's arguments, and reference() takes and returns one part's arrays. A program takes and returns all parts, laid end to end along the dimension named above; an argument that names none is the same for every part. Nothing has to cross between parts.
Inputs may be any that keep to these rules, and one draw needn't show every extreme that they name: `live_counts`: some attention rank holds exactly 8 live requests. `cache_lengths`: some request has exactly 256 cached keys.
All inputs are finite; a program needn't handle non-finite values.
Results may differ from the reference program's by a relative error of at most 0.0065.
Values may be sent and summed in bfloat16 or wider, within the bound.
A program may use at most 128 MiB of HBM per device.

```python
import jax
import jax.numpy as jnp
from jax import lax

D = 4096
HEADS = 32
KVH = 4
HD = 128
FF = 14336
STEPS = 2
RMAX = 8
LMAX = 256
RANKS = 16
REQS = 128


def shared_layout(key):
    positions = jax.random.randint(jax.random.fold_in(key, 101), (REQS,), LMAX, 4 * LMAX)
    strength_table = jnp.array([0.0, 0.0, 3.5, 4.0, 5.0], jnp.float32)
    pick_index = jax.random.randint(jax.random.fold_in(key, 102), (REQS, KVH), 0, 5)
    strengths = strength_table[pick_index]
    sign_pattern = jnp.where(jax.random.bernoulli(jax.random.fold_in(key, 103), 0.5, (REQS, KVH, HD)), 1.0, -1.0)
    return (positions, strengths, sign_pattern)


def draw_positions(key, part):
    layout = shared_layout(key)
    return layout[0].astype(jnp.int32)


def draw_queries(key, part):
    key = jax.random.fold_in(key, 1)
    group_size = HEADS // KVH
    base_values = jnp.clip(jax.random.normal(key, (REQS, STEPS, KVH, group_size, HD), jnp.float32), -6.0, 6.0)
    return base_values.reshape(REQS, STEPS, HEADS * HD).astype(jnp.bfloat16)


def draw_key_cache(key, part):
    key = jax.random.fold_in(key, 2)
    base_values = jnp.clip(jax.random.normal(key, (REQS, LMAX, KVH, HD), jnp.float32), -6.0, 6.0)
    return base_values.reshape(REQS, LMAX, KVH * HD).astype(jnp.bfloat16)


def draw_residual_in(key, part):
    key = jax.random.fold_in(key, 3)
    row_scale = jnp.exp(jax.random.uniform(jax.random.fold_in(key, 31), (REQS, STEPS, 1), jnp.float32, jnp.log(0.3), jnp.log(3.0)))
    column_scale = jnp.exp(jax.random.uniform(jax.random.fold_in(key, 32), (D,), jnp.float32, jnp.log(0.3), jnp.log(3.0)))
    base_values = jnp.clip(jax.random.normal(key, (REQS, STEPS, D), jnp.float32), -4.0, 4.0)
    return (base_values * row_scale * column_scale).astype(jnp.bfloat16)


def draw_live_counts(key, part):
    key = jax.random.fold_in(key, 4)
    lowest = max(1, RMAX - max(1, RMAX // 4))
    counts = jax.random.randint(key, (RANKS,), lowest, RMAX + 1)
    full_rank = jax.random.randint(jax.random.fold_in(key, 41), (), 0, RANKS)
    return jnp.where(jnp.arange(RANKS) == full_rank, RMAX, counts).astype(jnp.int32)


def draw_cache_lengths(key, part):
    key = jax.random.fold_in(key, 5)
    lengths = jax.random.randint(key, (REQS,), 2, LMAX + 1)
    full_request = jax.random.randint(jax.random.fold_in(key, 51), (), 0, REQS)
    return jnp.where(jnp.arange(REQS) == full_request, LMAX, lengths).astype(jnp.int32)


def level_of(own_key, shape, shards, smallest, largest):
    def one(axis_at, blocks):
        draws = jax.random.uniform(jax.random.fold_in(jax.random.fold_in(own_key, 6), axis_at), (blocks,), jnp.float32, smallest / len(shards), largest / len(shards))
        return jnp.repeat(jnp.exp(draws), shape[axis_at] // blocks).reshape((-1,) + (1,) * (len(shape) - axis_at - 1))

    gain = one(*shards[0])
    for cut in shards[1:]:
        gain = gain * one(*cut)
    return gain


def bell_draw(rng, shape, scale, most, shards=(), kind=jnp.bfloat16):
    result = jax.random.normal(rng, shape, jnp.float32) * scale
    if len(shards) > 0:
        result = level_of(rng, shape, shards, -0.22, 0.18) * result
    return jnp.clip(result, min=-most, max=most).astype(kind)


def setup_inputs(seed: int = 0, part: int = 0) -> dict:
    key_list = jax.random.split(jax.random.key(seed), 14)
    part_splits = jax.random.split(jax.random.fold_in(key_list[13], part), 14)
    queries = draw_queries(jax.random.fold_in(jax.random.fold_in(key_list[13], part), 71), part)
    new_keys = bell_draw(part_splits[1], (REQS, STEPS, KVH * HD), 1.0, 6.0, ((0, 16),))
    new_values = bell_draw(part_splits[2], (REQS, STEPS, KVH * HD), 1.0, 6.0, ((0, 16),))
    key_cache = draw_key_cache(jax.random.fold_in(jax.random.fold_in(key_list[13], part), 71), part)
    value_cache = bell_draw(part_splits[4], (REQS, LMAX, KVH * HD), 1.0, 6.0, ((0, 16),))
    residual_in = draw_residual_in(jax.random.fold_in(jax.random.fold_in(key_list[13], part), 71), part)
    norm_gain = jnp.clip(1.0 + 0.18 * jax.random.normal(key_list[6], (D,), jnp.float32), 0.099609375, 1.8984375).astype(jnp.bfloat16)
    gate_weight = bell_draw(key_list[7], (D, FF), D ** -0.5, 0.09375, ((1, 16),))
    up_weight = bell_draw(key_list[8], (D, FF), D ** -0.5, 0.09375, ((1, 16),))
    down_weight = bell_draw(key_list[9], (FF, D), FF ** -0.5, 0.046875, ((0, 16),))
    live_counts = draw_live_counts(jax.random.fold_in(jax.random.fold_in(key_list[13], part), 71), part)
    cache_lengths = draw_cache_lengths(jax.random.fold_in(jax.random.fold_in(key_list[13], part), 71), part)
    positions = draw_positions(jax.random.fold_in(jax.random.fold_in(key_list[13], part), 71), part)
    return dict(queries=queries, new_keys=new_keys, new_values=new_values, key_cache=key_cache, value_cache=value_cache, residual_in=residual_in, norm_gain=norm_gain, gate_weight=gate_weight, up_weight=up_weight, down_weight=down_weight, live_counts=live_counts, cache_lengths=cache_lengths, positions=positions)


rope_base = 500000.0
norm_epsilon = 1e-05

def rotate_heads(values, angles):
    middle = values.shape[-1] // 2
    cosine = jnp.cos(angles)
    sine = jnp.sin(angles)
    first = values[..., :middle]
    second = values[..., middle:]
    return jnp.concatenate([first * cosine - second * sine, second * cosine + first * sine], axis=-1)

def attend(queries, new_keys, new_values, key_cache, value_cache, cache_lengths, positions):
    requests = queries.shape[0]
    drafts = queries.shape[1]
    cache_slots = key_cache.shape[1]
    group_size = HEADS // KVH
    frequency = rope_base ** (-2.0 * jnp.arange(HD // 2, dtype=jnp.float32) / HD)
    offsets = positions.astype(jnp.float32)[:, None] + jnp.arange(drafts, dtype=jnp.float32)[None, :]
    angles = offsets[:, :, None, None] * frequency
    rotated_queries = rotate_heads(queries.astype(jnp.float32).reshape(requests, drafts, HEADS, HD), angles)
    rotated_queries = lax.optimization_barrier(rotated_queries.astype(jnp.bfloat16))
    rotated_queries = rotated_queries.reshape(requests, drafts, KVH, group_size, HD)
    rotated_keys = rotate_heads(new_keys.astype(jnp.float32).reshape(requests, drafts, KVH, HD), angles)
    rotated_keys = lax.optimization_barrier(rotated_keys.astype(jnp.bfloat16))
    cached_keys = key_cache.reshape(requests, cache_slots, KVH, HD)
    cached_values = value_cache.reshape(requests, cache_slots, KVH, HD)
    fresh_values = new_values.reshape(requests, drafts, KVH, HD)
    score_scale = HD ** (-0.5)
    cache_scores = jnp.einsum('rsgqd,rlgd->rgsql', rotated_queries.astype(jnp.float32), cached_keys.astype(jnp.float32)) * score_scale
    draft_scores = jnp.einsum('rsgqd,rtgd->rgsqt', rotated_queries.astype(jnp.float32), rotated_keys.astype(jnp.float32)) * score_scale
    cache_mask = (jnp.arange(cache_slots)[None, :] < cache_lengths[:, None])[:, None, None, None, :]
    draft_mask = (jnp.arange(drafts)[None, :] <= jnp.arange(drafts)[:, None])[None, None, :, None, :]
    cache_scores = jnp.where(cache_mask, cache_scores, -jnp.inf)
    draft_scores = jnp.where(draft_mask, draft_scores, -jnp.inf)
    highest = jnp.maximum(lax.optimization_barrier(jnp.max(cache_scores, axis=-1)), lax.optimization_barrier(jnp.max(draft_scores, axis=-1)))[..., None]
    cache_exp = jnp.exp(cache_scores - highest)
    draft_exp = jnp.exp(draft_scores - highest)
    denominator = lax.optimization_barrier(jnp.sum(cache_exp, axis=-1, keepdims=True)) + lax.optimization_barrier(jnp.sum(draft_exp, axis=-1, keepdims=True))
    cache_weights = lax.optimization_barrier((cache_exp / denominator).astype(jnp.bfloat16))
    draft_weights = lax.optimization_barrier((draft_exp / denominator).astype(jnp.bfloat16))
    mixed = jnp.einsum('rgsql,rlgd->rsgqd', cache_weights.astype(jnp.float32), cached_values.astype(jnp.float32))
    mixed = mixed + jnp.einsum('rgsqt,rtgd->rsgqd', draft_weights.astype(jnp.float32), fresh_values.astype(jnp.float32))
    return mixed.reshape(requests, drafts, HEADS * HD)

def normalize(stream, norm_gain):
    values = stream.astype(jnp.float32)
    mean_square = lax.optimization_barrier(jnp.mean(values * values, axis=-1, keepdims=True))
    return (values * lax.rsqrt(mean_square + norm_epsilon) * norm_gain.astype(jnp.float32)).astype(jnp.bfloat16)

def feed_forward_rows(picked, gate_weight, up_weight, down_weight):
    gate_proj = jnp.dot(picked, gate_weight, preferred_element_type=jnp.float32)
    up_proj = jnp.dot(picked, up_weight, preferred_element_type=jnp.float32)
    hidden = (jax.nn.silu(gate_proj) * up_proj).astype(jnp.bfloat16)
    return jnp.dot(hidden, down_weight, preferred_element_type=jnp.float32)

def reference(queries, new_keys, new_values, key_cache, value_cache, residual_in, norm_gain, gate_weight, up_weight, down_weight, live_counts, cache_lengths, positions):
    attention = attend(queries, new_keys, new_values, key_cache, value_cache, cache_lengths, positions)
    stream = lax.optimization_barrier((residual_in.astype(jnp.float32) + attention).astype(jnp.bfloat16))
    normed = normalize(stream, norm_gain).reshape(REQS * STEPS, D)
    feed = feed_forward_rows(normed, gate_weight, up_weight, down_weight).reshape(REQS, STEPS, D)
    live_slot = jnp.arange(REQS) % RMAX < jnp.repeat(live_counts, RMAX)
    combined = (stream.astype(jnp.float32) + feed).astype(jnp.bfloat16)
    return jnp.where(live_slot[:, None, None], combined, jnp.zeros_like(combined))
```

```python
import functools

import jax
import jax.numpy as jnp
from jax import lax
from jax.experimental import pallas as pl
from jax.experimental.pallas import tpu as pltpu
from jax.sharding import PartitionSpec as P

HEADS = 32
KVH = 4
HD = 128


rope_base = 500000.0
norm_epsilon = 1e-05

MESH = pl.DeviceIdType.MESH
UP, DOWN, SIDE, CORE = range(4)


def rotate_heads(values, angles):
    middle = values.shape[-1] // 2
    cosine = jnp.cos(angles)
    sine = jnp.sin(angles)
    first = values[..., :middle]
    second = values[..., middle:]
    return jnp.concatenate(
        [first * cosine - second * sine, second * cosine + first * sine], axis=-1
    )


def attend_kernel(
    C, lengths_ref, q_ref, dk_ref, dv_ref, k_ref, v_ref, residual_ref, gain_ref,
    stream_ref, normed_ref, mixed_ref,
):
    r = pl.program_id(0)
    requests = pl.num_programs(0)
    slots = k_ref.shape[1]
    group = HEADS // KVH
    q = q_ref[0]
    scale = HD ** (-0.5)
    scores = jnp.concatenate(
        [
            lax.dot_general(
                q[g * 2 * group : (g + 1) * 2 * group],
                k_ref[0, :, g * HD : (g + 1) * HD],
                (((1,), (1,)), ((), ())),
                preferred_element_type=jnp.float32,
            )
            for g in range(KVH)
        ],
        axis=0,
    ) * scale
    rows = 2 * HEADS
    inside = lax.broadcasted_iota(jnp.int32, (rows, slots), 1) < lengths_ref[r]
    scores = jnp.where(inside, scores, -jnp.inf)

    def spread(ref, t):
        part = ref[0, t].astype(jnp.float32)
        return jnp.concatenate(
            [jnp.broadcast_to(part[g : g + 1], (2 * group, HD)) for g in range(KVH)], axis=0
        )

    wide = q.astype(jnp.float32)
    first = jnp.sum(wide * spread(dk_ref, 0), axis=-1, keepdims=True) * scale
    second = jnp.sum(wide * spread(dk_ref, 1), axis=-1, keepdims=True) * scale
    late = (lax.broadcasted_iota(jnp.int32, (rows, 1), 0) // group) % 2 == 1
    second = jnp.where(late, second, -jnp.inf)
    highest = jnp.maximum(jnp.max(scores, axis=-1, keepdims=True), jnp.maximum(first, second))
    scores = jnp.exp(scores - highest)
    first = jnp.exp(first - highest)
    second = jnp.exp(second - highest)
    total = jnp.sum(scores, axis=-1, keepdims=True) + first + second
    weights = (scores / total).astype(jnp.bfloat16)
    first = (first / total).astype(jnp.bfloat16).astype(jnp.float32)
    second = (second / total).astype(jnp.bfloat16).astype(jnp.float32)
    extra = first * spread(dv_ref, 0) + second * spread(dv_ref, 1)
    for g in range(KVH):
        at = slice(g * 2 * group, (g + 1) * 2 * group)
        mixed = extra[at] + jnp.dot(
            weights[at], v_ref[0, :, g * HD : (g + 1) * HD], preferred_element_type=jnp.float32
        )
        for s in range(2):
            start = pl.multiple_of((r * 2 + s) * HEADS, 8) + g * group
            mixed_ref[pl.ds(start, group), :] = mixed[s * group : (s + 1) * group]

    @pl.when(r == requests - 1)
    def _():
        count = residual_ref.shape[0]
        square = jnp.zeros((count, HD), jnp.float32)
        for h in range(HEADS):
            at = slice(h * HD, (h + 1) * HD)
            value = residual_ref[:, at].astype(jnp.float32) + mixed_ref[pl.ds(h, count, stride=HEADS), :]
            value = value.astype(jnp.bfloat16)
            stream_ref[:, at] = value
            value = value.astype(jnp.float32)
            square += value * value
        mean = jnp.sum(square, axis=-1, keepdims=True) / (HEADS * HD)
        factor = lax.rsqrt(mean + norm_epsilon)
        width = normed_ref.shape[2]
        for k in range(C):
            at = slice(k * width, (k + 1) * width)
            normed_ref[k] = (
                stream_ref[:, at].astype(jnp.float32) * factor * gain_ref[:, at].astype(jnp.float32)
            ).astype(jnp.bfloat16)


def attend(C, queries, new_keys, new_values, key_cache, value_cache, residual, gain, lengths, positions):
    requests, drafts = queries.shape[:2]
    slots = key_cache.shape[1]
    group = HEADS // KVH
    frequency = rope_base ** (-2.0 * jnp.arange(HD // 2, dtype=jnp.float32) / HD)
    offsets = (
        positions.astype(jnp.float32)[:, None] + jnp.arange(drafts, dtype=jnp.float32)[None, :]
    )
    angles = offsets[:, :, None, None] * frequency
    q = rotate_heads(queries.astype(jnp.float32).reshape(requests, drafts, HEADS, HD), angles)
    q = q.astype(jnp.bfloat16).reshape(requests, drafts, KVH, group, HD)
    q = q.transpose(0, 2, 1, 3, 4).reshape(requests, KVH * drafts * group, HD)
    dk = rotate_heads(new_keys.astype(jnp.float32).reshape(requests, drafts, KVH, HD), angles)
    dk = dk.astype(jnp.bfloat16)
    dv = new_values.reshape(requests, drafts, KVH, HD)
    count = requests * drafts
    width = HEADS * HD
    return pl.pallas_call(
        functools.partial(attend_kernel, C),
        grid=(requests,),
        in_specs=[
            pl.BlockSpec(memory_space=pltpu.SMEM),
            pl.BlockSpec((1, 2 * HEADS, HD), lambda r: (r, 0, 0)),
            pl.BlockSpec((1, drafts, KVH, HD), lambda r: (r, 0, 0, 0)),
            pl.BlockSpec((1, drafts, KVH, HD), lambda r: (r, 0, 0, 0)),
            pl.BlockSpec((1, slots, KVH * HD), lambda r: (r, 0, 0)),
            pl.BlockSpec((1, slots, KVH * HD), lambda r: (r, 0, 0)),
            pl.BlockSpec((count, width), lambda r: (0, 0)),
            pl.BlockSpec((1, width), lambda r: (0, 0)),
        ],
        out_specs=[
            pl.BlockSpec((count, width), lambda r: (0, 0)),
            pl.BlockSpec((C, count, width // C), lambda r: (0, 0, 0)),
        ],
        out_shape=[
            jax.ShapeDtypeStruct((count, width), jnp.bfloat16),
            jax.ShapeDtypeStruct((C, count, width // C), jnp.bfloat16),
        ],
        scratch_shapes=[pltpu.VMEM((count * HEADS, HD), jnp.float32)],
        cost_estimate=pl.CostEstimate(flops=10**8, bytes_accessed=5 * 10**6, transcendentals=10**5),
    )(lengths, q, dk, dv, key_cache, value_cache, residual, gain)


def feed_kernel(
    C, Z, Y, normed_ref, stream_ref, wg_hbm, wu_hbm, wd_hbm, out_ref,
    gath, wg, wu, wd, acc_g, acc_u, hid, part, r_core, r_side, r_line, fin,
    w_sem, ag_send, ag_recv, core_send, core_recv, side_send, side_recv, line_send, line_recv,
):
    c = lax.axis_index("attn")
    f = lax.axis_index("ffn")
    z, y = f // Y, f % Y
    R = stream_ref.shape[0]
    N = 2 * Y * Z
    kc = gath.shape[2]
    width = part.shape[2]
    up = {"ffn": (z + 1) * Y + y}
    down = {"ffn": (z - 1) * Y + y}
    side = {"ffn": z * Y + (Y - 1 - y)}
    core = {"attn": 1 - c}
    targets = [up, down, side, core]
    has_up, has_down = z < Z - 1, z > 0

    weight_copies = []
    for k in range(C):
        at = pl.ds(k * kc, kc)
        weight_copies.append(pltpu.make_async_copy(wg_hbm.at[at, :], wg.at[at, :], w_sem.at[0, k]))
        weight_copies.append(pltpu.make_async_copy(wu_hbm.at[at, :], wu.at[at, :], w_sem.at[1, k]))
    for n in range(C):
        at = pl.ds(n * width, width)
        weight_copies.append(pltpu.make_async_copy(wd_hbm.at[:, at], wd.at[:, at], w_sem.at[2, n]))
    for copy in weight_copies:
        copy.start()

    barrier = pltpu.get_barrier_semaphore()

    def greet(target):
        pl.semaphore_signal(barrier, inc=1, device_id=target, device_id_type=MESH)

    greet(core)
    if Y == 2:
        greet(side)
    pl.when(has_up)(lambda: greet(up))
    pl.when(has_down)(lambda: greet(down))

    def index(cc, yy, zz):
        return (cc * Y + yy) * Z + zz

    def rows(at, count=1):
        return pl.ds(pl.multiple_of(at * R, R), count * R)

    own = index(c, y, z)
    for k in range(C):
        gath[k, rows(own), :] = normed_ref[k]

    peers = 2 if Y == 2 else 1
    ends = jnp.logical_or(z == 0, z == Z - 1)
    pl.when(ends)(lambda: pl.semaphore_wait(barrier, peers + 1))
    pl.when(jnp.logical_not(ends))(lambda: pl.semaphore_wait(barrier, peers + 2))

    def ag(k, block, way):
        at = gath.at[k, rows(block), :]
        return pltpu.make_async_remote_copy(
            src_ref=at, dst_ref=at, send_sem=ag_send.at[way, k, block],
            recv_sem=ag_recv.at[k, block], device_id=targets[way], device_id_type=MESH,
        )

    def line_step(d, k, act):
        if d == 0:
            pl.when(has_up)(lambda: act(k, own, UP))
            pl.when(has_down)(lambda: act(k, own, DOWN))
            if Y == 2:
                act(k, own, SIDE)
            act(k, own, CORE)
            return

        def arrived(block, way, more):
            if act is start:
                ag(k, block, way).wait_recv()
            pl.when(more)(lambda: act(k, block, way))
            if Y == 2:
                act(k, block, SIDE)
            act(k, block, CORE)

        pl.when(z - d >= 0)(lambda: arrived(index(c, y, z - d), UP, has_up))
        pl.when(z + d < Z)(lambda: arrived(index(c, y, z + d), DOWN, has_down))

    def side_step(d, k, act):
        def arrived(block):
            if act is start:
                ag(k, block, SIDE).wait_recv()
            act(k, block, CORE)

        if d == 0:
            arrived(index(c, 1 - y, z))
        else:
            pl.when(z - d >= 0)(lambda: arrived(index(c, 1 - y, z - d)))
            pl.when(z + d < Z)(lambda: arrived(index(c, 1 - y, z + d)))

    def start(k, block, way):
        ag(k, block, way).start()

    def finish(k, block, way):
        ag(k, block, way).wait_send()

    def project(k):
        for j in range(Y * Z):
            ag(k, (1 - c) * Y * Z + j, CORE).wait_recv()
        weight_copies[2 * k].wait()
        weight_copies[2 * k + 1].wait()
        at = pl.ds(k * kc, kc)
        ff = wg.shape[1]
        x = gath[k]
        if ff % 128 == 0:
            both = jnp.concatenate([wg[at, :], wu[at, :]], axis=1)
            both = jnp.dot(x, both, preferred_element_type=jnp.float32)
            new_g, new_u = both[:, :ff], both[:, ff:]
        else:
            new_g = jnp.dot(x, wg[at, :], preferred_element_type=jnp.float32)
            new_u = jnp.dot(x, wu[at, :], preferred_element_type=jnp.float32)
        if k > 0:
            new_g = acc_g[...] + new_g
            new_u = acc_u[...] + new_u
        if k < C - 1:
            acc_g[...] = new_g
            acc_u[...] = new_u
        else:
            hid[...] = (new_g / (1.0 + jnp.exp(-new_g)) * new_u).astype(jnp.bfloat16)

    lag = 2
    for t in range(C + Z + lag):
        for d in range(Z):
            if 0 <= t - d < C:
                line_step(d, t - d, start)
        if Y == 2:
            for d in range(Z):
                if 0 <= t - lag - d < C:
                    side_step(d, t - lag - d, start)
        k = t - lag - (Z - 1)
        if 0 <= k < C:
            project(k)

    half = Y * Z

    def core_copy(n):
        return pltpu.make_async_remote_copy(
            src_ref=part.at[n, rows((1 - c) * half, half), :], dst_ref=r_core.at[n],
            send_sem=core_send.at[n], recv_sem=core_recv.at[n],
            device_id=core, device_id_type=MESH,
        )

    def side_copy(n):
        return pltpu.make_async_remote_copy(
            src_ref=part.at[n, rows(index(c, 1 - y, 0), Z), :], dst_ref=r_side.at[n],
            send_sem=side_send.at[n], recv_sem=side_recv.at[n],
            device_id=side, device_id_type=MESH,
        )

    def line_copy(n, goal, way):
        slot = goal + 1 if way == UP else goal
        return pltpu.make_async_remote_copy(
            src_ref=part.at[n, rows(index(c, y, goal)), :], dst_ref=r_line.at[n, rows(slot), :],
            send_sem=line_send.at[n, goal], recv_sem=line_recv.at[n, slot],
            device_id=targets[way], device_id_type=MESH,
        )

    def add(n, at, other):
        part[n, at, :] = (
            part[n, at, :].astype(jnp.float32) + other.astype(jnp.float32)
        ).astype(jnp.bfloat16)

    def produce(n):
        weight_copies[2 * C + n].wait()
        at = pl.ds(n * width, width)
        part[n] = jnp.dot(
            hid[...], wd[:, at], preferred_element_type=jnp.float32
        ).astype(jnp.bfloat16)
        core_copy(n).start()

    def after_core(n):
        core_copy(n).wait_recv()
        if Y == 2:
            add(n, rows(index(c, 1 - y, 0), Z), r_core[n, rows((1 - y) * Z, Z), :])
            side_copy(n).start()
        add(n, rows(index(c, y, 0), Z), r_core[n, rows(y * Z, Z), :])

    def after_side(n):
        if Y == 2:
            side_copy(n).wait_recv()
            add(n, rows(index(c, y, 0), Z), r_side[n])

    def along(n, way):
        source = has_down if way == UP else has_up
        for step in range(Z - 1):
            goal = Z - 1 - step if way == UP else step

            def move(goal=goal):
                @pl.when(source)
                def _():
                    line_copy(n, goal, way).wait_recv()
                    slot = goal + 1 if way == UP else goal
                    add(n, rows(index(c, y, goal)), r_line[n, rows(slot), :])

                line_copy(n, goal, way).start()

            pl.when(goal > z if way == UP else goal < z)(move)

    def complete(n):
        at = pl.ds(n * width, width)
        fin[...] = part[n, rows(own), :].astype(jnp.float32)

        @pl.when(has_down)
        def _():
            line_copy(n, z, UP).wait_recv()
            fin[...] += r_line[n, rows(z + 1), :].astype(jnp.float32)

        @pl.when(has_up)
        def _():
            line_copy(n, z, DOWN).wait_recv()
            fin[...] += r_line[n, rows(z), :].astype(jnp.float32)

        out_ref[:, at] = (stream_ref[:, at].astype(jnp.float32) + fin[...]).astype(jnp.bfloat16)

    if C == 1:
        produce(0)
        after_core(0)
        after_side(0)
        along(0, UP)
        along(0, DOWN)
        complete(0)
    else:
        for t in range(C + Z + 4):
            if t < C:
                produce(t)
            if 0 <= t - 1 < C:
                after_core(t - 1)
            if 0 <= t - 2 < C:
                after_side(t - 2)
            for hop in range(Z - 1):
                n = t - 2 - hop
                if 0 <= n < C:
                    pl.when(z == hop)(functools.partial(along, n, UP))
                    pl.when(z == Z - 1 - hop)(functools.partial(along, n, DOWN))
            if 0 <= t - 2 - Z < C:
                complete(t - 2 - Z)

    for k in range(C):
        for d in range(Z):
            line_step(d, k, finish)
            if Y == 2:
                side_step(d, k, finish)
        core_copy(k).wait_send()
        if Y == 2:
            side_copy(k).wait_send()
        for goal in range(Z):
            pl.when(goal > z)(lambda goal=goal: line_copy(k, goal, UP).wait_send())
            pl.when(goal < z)(lambda goal=goal: line_copy(k, goal, DOWN).wait_send())


def feed(C, Z, Y, normed, stream, wg, wu, wd):
    R, D = stream.shape
    ff = wg.shape[1]
    N = 2 * Y * Z
    M = N * R
    width = D // C
    bf16 = jnp.bfloat16
    dma = pltpu.SemaphoreType.DMA
    vmem = pl.BlockSpec(memory_space=pltpu.VMEM)
    hbm = pl.BlockSpec(memory_space=pl.ANY)
    return pl.pallas_call(
        functools.partial(feed_kernel, C, Z, Y),
        out_shape=jax.ShapeDtypeStruct((R, D), bf16),
        in_specs=[vmem, vmem, hbm, hbm, hbm],
        out_specs=vmem,
        scratch_shapes=[
            pltpu.VMEM((C, M, width), bf16),
            pltpu.VMEM((D, ff), bf16),
            pltpu.VMEM((D, ff), bf16),
            pltpu.VMEM((ff, D), bf16),
            pltpu.VMEM((M, ff), jnp.float32),
            pltpu.VMEM((M, ff), jnp.float32),
            pltpu.VMEM((M, ff), bf16),
            pltpu.VMEM((C, M, width), bf16),
            pltpu.VMEM((C, M // 2, width), bf16),
            pltpu.VMEM((C, Z * R, width), bf16),
            pltpu.VMEM((C, (Z + 1) * R, width), bf16),
            pltpu.VMEM((R, width), jnp.float32),
            dma((3, C)),
            dma((4, C, N)),
            dma((C, N)),
            dma((C,)),
            dma((C,)),
            dma((C,)),
            dma((C,)),
            dma((C, Z)),
            dma((C, Z + 1)),
        ],
        compiler_params=pltpu.CompilerParams(
            collective_id=0, has_side_effects=True, vmem_limit_bytes=58 * 1024 * 1024
        ),
        cost_estimate=pl.CostEstimate(
            flops=6 * M * D * ff, bytes_accessed=6 * D * ff, transcendentals=M * ff
        ),
    )(normed, stream, wg, wu, wd)


def shards(
    Z,
    Y,
    C,
    queries,
    new_keys,
    new_values,
    key_cache,
    value_cache,
    residual_in,
    norm_gain,
    gate_weight,
    up_weight,
    down_weight,
    live_counts,
    cache_lengths,
    positions,
):
    requests, drafts, width = residual_in.shape
    stream, normed = attend(
        C, queries, new_keys, new_values, key_cache, value_cache,
        residual_in.reshape(requests * drafts, width), norm_gain.reshape(1, width),
        cache_lengths, positions,
    )
    combined = feed(C, Z, Y, normed, stream, gate_weight, up_weight, down_weight)
    combined = combined.reshape(requests, drafts, width)
    live_slot = jnp.arange(requests) < live_counts[0]
    return jnp.where(live_slot[:, None, None], combined, jnp.zeros_like(combined))


def solution(mesh):
    ffn = mesh.shape["ffn"]
    Y = 2 if ffn % 2 == 0 and ffn <= 8 else 1
    C = 4 if ffn <= 8 else 1
    return jax.shard_map(
        functools.partial(shards, ffn // Y, Y, C),
        mesh=mesh,
        in_specs=(
            P(("rep", "attn", "ffn"), None, None),
            P(("rep", "attn", "ffn"), None, None),
            P(("rep", "attn", "ffn"), None, None),
            P(("rep", "attn", "ffn"), None, None),
            P(("rep", "attn", "ffn"), None, None),
            P(("rep", "attn", "ffn"), None, None),
            P(),
            P(None, ("attn", "ffn")),
            P(None, ("attn", "ffn")),
            P(("attn", "ffn"), None),
            P(("rep", "attn", "ffn")),
            P(("rep", "attn", "ffn")),
            P(("rep", "attn", "ffn")),
        ),
        out_specs=P(("rep", "attn", "ffn"), None, None),
        check_vma=False,
    )
```

```python
import functools

import jax
import jax.numpy as jnp
from jax import lax
from jax.experimental import pallas as pl
from jax.experimental.pallas import tpu as pltpu
from jax.sharding import PartitionSpec as P

HEADS = 32
KVH = 4
HD = 128


rope_base = 500000.0
norm_epsilon = 1e-05

MESH = pl.DeviceIdType.MESH
UP, DOWN, SIDE, CORE = range(4)


def attend_kernel(
    C, batch, lengths_ref, q_ref, dk_ref, dv_ref, k_ref, v_ref, residual_ref, gain_ref, cos_ref, sin_ref,
    stream_ref, normed_ref, wide_ref, heads_ref, mixed_ref,
):
    step = pl.program_id(0)
    slots = k_ref.shape[1]
    requests = q_ref.shape[0]
    count = 2 * requests
    group = HEADS // KVH
    scale = HD ** (-0.5)
    rows = 2 * HEADS

    def widen(ref):
        for r in range(requests):
            wide_ref[2 * r : 2 * r + 2, :] = ref[r].astype(jnp.float32)

    def rotate(value, cosine, sine):
        return value * cosine + pltpu.roll(value, HD // 2, 1) * sine

    @pl.when(step == 0)
    def _():
        widen(q_ref)
        for h in range(HEADS):
            value = rotate(wide_ref[:, h * HD : (h + 1) * HD], cos_ref[...], sin_ref[...])
            heads_ref[pl.ds(h, count, stride=HEADS), :] = value
        widen(residual_ref)

    late = (lax.broadcasted_iota(jnp.int32, (rows, 1), 0) // group) % 2 == 1
    column = lax.broadcasted_iota(jnp.int32, (rows, slots), 1)

    def spread(part, t):
        return jnp.concatenate(
            [
                jnp.broadcast_to(part[t : t + 1, g * HD : (g + 1) * HD], (2 * group, HD))
                for g in range(KVH)
            ],
            axis=0,
        )

    picked = []
    for b in range(batch):
        r = step * batch + b
        first_row = pl.multiple_of(r * rows, 8)
        q = jnp.concatenate(
            [
                heads_ref[pl.ds(first_row + s * HEADS + g * group, group), :]
                for g in range(KVH)
                for s in range(2)
            ],
            axis=0,
        ).astype(jnp.bfloat16)
        scores = jnp.concatenate(
            [
                lax.dot_general(
                    q[g * 2 * group : (g + 1) * 2 * group],
                    k_ref[b, :, g * HD : (g + 1) * HD],
                    (((1,), (1,)), ((), ())),
                    preferred_element_type=jnp.float32,
                )
                for g in range(KVH)
            ],
            axis=0,
        ) * scale
        scores = jnp.where(column < lengths_ref[r], scores, -jnp.inf)
        cosine, sine = cos_ref[pl.ds(2 * r, 2), :], sin_ref[pl.ds(2 * r, 2), :]
        fresh = dk_ref[b].astype(jnp.float32)
        fresh = jnp.concatenate(
            [rotate(fresh[:, g * HD : (g + 1) * HD], cosine, sine) for g in range(KVH)], axis=1
        ).astype(jnp.bfloat16).astype(jnp.float32)
        wide = q.astype(jnp.float32)
        first = jnp.sum(wide * spread(fresh, 0), axis=-1, keepdims=True) * scale
        second = jnp.sum(wide * spread(fresh, 1), axis=-1, keepdims=True) * scale
        second = jnp.where(late, second, -jnp.inf)
        picked.append((r, scores, first, second))

    for b in range(batch):
        r, scores, first, second = picked[b]
        highest = jnp.maximum(jnp.max(scores, axis=-1, keepdims=True), jnp.maximum(first, second))
        scores = jnp.exp(scores - highest)
        first = jnp.exp(first - highest)
        second = jnp.exp(second - highest)
        total = 1.0 / (jnp.sum(scores, axis=-1, keepdims=True) + first + second)
        weights = (scores * total).astype(jnp.bfloat16)
        first = (first * total).astype(jnp.bfloat16).astype(jnp.float32)
        second = (second * total).astype(jnp.bfloat16).astype(jnp.float32)
        fresh = dv_ref[b].astype(jnp.float32)
        extra = first * spread(fresh, 0) + second * spread(fresh, 1)
        first_row = pl.multiple_of(r * rows, 8)
        for g in range(KVH):
            at = slice(g * 2 * group, (g + 1) * 2 * group)
            mixed = extra[at] + jnp.dot(
                weights[at], v_ref[b, :, g * HD : (g + 1) * HD], preferred_element_type=jnp.float32
            )
            for s in range(2):
                mixed_ref[pl.ds(first_row + s * HEADS + g * group, group), :] = mixed[
                    s * group : (s + 1) * group
                ]

    @pl.when(step == pl.num_programs(0) - 1)
    def _():
        square = jnp.zeros((count, HD), jnp.float32)
        for h in range(HEADS):
            at = slice(h * HD, (h + 1) * HD)
            value = wide_ref[:, at] + mixed_ref[pl.ds(h, count, stride=HEADS), :]
            value = value.astype(jnp.bfloat16)
            stream_ref[:, at] = value
            value = value.astype(jnp.float32)
            square += value * value
        mean = jnp.sum(square, axis=-1, keepdims=True) / (HEADS * HD)
        factor = lax.rsqrt(mean + norm_epsilon)
        width = normed_ref.shape[2]
        for k in range(C):
            at = slice(k * width, (k + 1) * width)
            normed_ref[k] = (
                stream_ref[:, at].astype(jnp.float32) * factor * gain_ref[at].astype(jnp.float32)[None, :]
            ).astype(jnp.bfloat16)


def attend(C, queries, new_keys, new_values, key_cache, value_cache, residual, gain, lengths, positions):
    requests, drafts = queries.shape[:2]
    slots = key_cache.shape[1]
    count = requests * drafts
    width = HEADS * HD
    batch = 4 if requests % 4 == 0 else 1
    place = jnp.arange(HD)
    frequency = rope_base ** (-2.0 * (place % (HD // 2)).astype(jnp.float32) / HD)
    row = jnp.arange(count)
    offsets = jnp.repeat(positions, drafts).astype(jnp.float32) + (row % drafts).astype(jnp.float32)
    angles = offsets[:, None] * frequency[None, :]
    cosine = jnp.cos(angles)
    sine = jnp.where(place[None, :] < HD // 2, -jnp.sin(angles), jnp.sin(angles))
    whole = pl.BlockSpec(memory_space=pltpu.VMEM)
    return pl.pallas_call(
        functools.partial(attend_kernel, C, batch),
        grid=(requests // batch,),
        in_specs=[
            pl.BlockSpec(memory_space=pltpu.SMEM),
            whole,
            pl.BlockSpec((batch, drafts, KVH * HD), lambda r: (r, 0, 0)),
            pl.BlockSpec((batch, drafts, KVH * HD), lambda r: (r, 0, 0)),
            pl.BlockSpec((batch, slots, KVH * HD), lambda r: (r, 0, 0)),
            pl.BlockSpec((batch, slots, KVH * HD), lambda r: (r, 0, 0)),
            whole,
            whole,
            whole,
            whole,
        ],
        out_specs=[
            pl.BlockSpec((count, width), lambda r: (0, 0)),
            pl.BlockSpec((C, count, width // C), lambda r: (0, 0, 0)),
        ],
        out_shape=[
            jax.ShapeDtypeStruct((count, width), jnp.bfloat16),
            jax.ShapeDtypeStruct((C, count, width // C), jnp.bfloat16),
        ],
        scratch_shapes=[
            pltpu.VMEM((count, width), jnp.float32),
            pltpu.VMEM((count * HEADS, HD), jnp.float32),
            pltpu.VMEM((count * HEADS, HD), jnp.float32),
        ],
        compiler_params=pltpu.CompilerParams(vmem_limit_bytes=32 * 1024 * 1024),
        cost_estimate=pl.CostEstimate(flops=10**8, bytes_accessed=5 * 10**6, transcendentals=10**5),
    )(lengths, queries, new_keys, new_values, key_cache, value_cache, residual, gain, cosine, sine)


def feed_kernel(
    C, Z, Y, normed_ref, stream_ref, wg_hbm, wu_hbm, wd_hbm, out_ref,
    gath, wg, wu, wd, acc_g, acc_u, hid, part, r_core, r_side, r_line, fin,
    w_sem, ag_send, ag_recv, core_send, core_recv, side_send, side_recv, line_send, line_recv,
):
    c = lax.axis_index("attn")
    f = lax.axis_index("ffn")
    z, y = f // Y, f % Y
    R = stream_ref.shape[0]
    N = 2 * Y * Z
    kc = gath.shape[2]
    width = part.shape[2]
    up = {"ffn": (z + 1) * Y + y}
    down = {"ffn": (z - 1) * Y + y}
    side = {"ffn": z * Y + (Y - 1 - y)}
    core = {"attn": 1 - c}
    targets = [up, down, side, core]
    has_up, has_down = z < Z - 1, z > 0

    weight_copies = []
    for k in range(C):
        at = pl.ds(k * kc, kc)
        weight_copies.append(pltpu.make_async_copy(wg_hbm.at[at, :], wg.at[at, :], w_sem.at[0, k]))
        weight_copies.append(pltpu.make_async_copy(wu_hbm.at[at, :], wu.at[at, :], w_sem.at[1, k]))
    for n in range(C):
        at = pl.ds(n * width, width)
        weight_copies.append(pltpu.make_async_copy(wd_hbm.at[:, at], wd.at[:, at], w_sem.at[2, n]))
    for copy in weight_copies:
        copy.start()

    barrier = pltpu.get_barrier_semaphore()

    def greet(target):
        pl.semaphore_signal(barrier, inc=1, device_id=target, device_id_type=MESH)

    greet(core)
    if Y == 2:
        greet(side)
    pl.when(has_up)(lambda: greet(up))
    pl.when(has_down)(lambda: greet(down))

    def index(cc, yy, zz):
        return (cc * Y + yy) * Z + zz

    def rows(at, count=1):
        return pl.ds(pl.multiple_of(at * R, R), count * R)

    own = index(c, y, z)
    for k in range(C):
        gath[k, rows(own), :] = normed_ref[k]

    peers = 2 if Y == 2 else 1
    ends = jnp.logical_or(z == 0, z == Z - 1)
    pl.when(ends)(lambda: pl.semaphore_wait(barrier, peers + 1))
    pl.when(jnp.logical_not(ends))(lambda: pl.semaphore_wait(barrier, peers + 2))

    def ag(k, block, way):
        at = gath.at[k, rows(block), :]
        return pltpu.make_async_remote_copy(
            src_ref=at, dst_ref=at, send_sem=ag_send.at[way, k, block],
            recv_sem=ag_recv.at[k, block], device_id=targets[way], device_id_type=MESH,
        )

    def line_step(d, k, act):
        if d == 0:
            pl.when(has_up)(lambda: act(k, own, UP))
            pl.when(has_down)(lambda: act(k, own, DOWN))
            if Y == 2:
                act(k, own, SIDE)
            act(k, own, CORE)
            return

        def arrived(block, way, more):
            if act is start:
                ag(k, block, way).wait_recv()
            pl.when(more)(lambda: act(k, block, way))
            if Y == 2:
                act(k, block, SIDE)
            act(k, block, CORE)

        pl.when(z - d >= 0)(lambda: arrived(index(c, y, z - d), UP, has_up))
        pl.when(z + d < Z)(lambda: arrived(index(c, y, z + d), DOWN, has_down))

    def side_step(d, k, act):
        def arrived(block):
            if act is start:
                ag(k, block, SIDE).wait_recv()
            act(k, block, CORE)

        if d == 0:
            arrived(index(c, 1 - y, z))
        else:
            pl.when(z - d >= 0)(lambda: arrived(index(c, 1 - y, z - d)))
            pl.when(z + d < Z)(lambda: arrived(index(c, 1 - y, z + d)))

    def start(k, block, way):
        ag(k, block, way).start()

    def finish(k, block, way):
        ag(k, block, way).wait_send()

    def project(k):
        for j in range(Y * Z):
            ag(k, (1 - c) * Y * Z + j, CORE).wait_recv()
        weight_copies[2 * k].wait()
        weight_copies[2 * k + 1].wait()
        at = pl.ds(k * kc, kc)
        ff = wg.shape[1]
        x = gath[k]
        if ff % 128 == 0:
            both = jnp.concatenate([wg[at, :], wu[at, :]], axis=1)
            both = jnp.dot(x, both, preferred_element_type=jnp.float32)
            new_g, new_u = both[:, :ff], both[:, ff:]
        else:
            new_g = jnp.dot(x, wg[at, :], preferred_element_type=jnp.float32)
            new_u = jnp.dot(x, wu[at, :], preferred_element_type=jnp.float32)
        if k > 0:
            new_g = acc_g[...] + new_g
            new_u = acc_u[...] + new_u
        if k < C - 1:
            acc_g[...] = new_g
            acc_u[...] = new_u
        else:
            hid[...] = (new_g / (1.0 + jnp.exp(-new_g)) * new_u).astype(jnp.bfloat16)

    lag = 2
    for t in range(C + Z + lag):
        for d in range(Z):
            if 0 <= t - d < C:
                line_step(d, t - d, start)
        if Y == 2:
            for d in range(Z):
                if 0 <= t - lag - d < C:
                    side_step(d, t - lag - d, start)
        k = t - lag - (Z - 1)
        if 0 <= k < C:
            project(k)

    half = Y * Z

    def core_copy(n):
        return pltpu.make_async_remote_copy(
            src_ref=part.at[n, rows((1 - c) * half, half), :], dst_ref=r_core.at[n],
            send_sem=core_send.at[n], recv_sem=core_recv.at[n],
            device_id=core, device_id_type=MESH,
        )

    def side_copy(n):
        return pltpu.make_async_remote_copy(
            src_ref=part.at[n, rows(index(c, 1 - y, 0), Z), :], dst_ref=r_side.at[n],
            send_sem=side_send.at[n], recv_sem=side_recv.at[n],
            device_id=side, device_id_type=MESH,
        )

    def line_copy(n, goal, way):
        slot = goal + 1 if way == UP else goal
        return pltpu.make_async_remote_copy(
            src_ref=part.at[n, rows(index(c, y, goal)), :], dst_ref=r_line.at[n, rows(slot), :],
            send_sem=line_send.at[n, goal], recv_sem=line_recv.at[n, slot],
            device_id=targets[way], device_id_type=MESH,
        )

    def add(n, at, other):
        part[n, at, :] = (
            part[n, at, :].astype(jnp.float32) + other.astype(jnp.float32)
        ).astype(jnp.bfloat16)

    def produce(n):
        weight_copies[2 * C + n].wait()
        at = pl.ds(n * width, width)
        part[n] = jnp.dot(
            hid[...], wd[:, at], preferred_element_type=jnp.float32
        ).astype(jnp.bfloat16)
        core_copy(n).start()

    def after_core(n):
        core_copy(n).wait_recv()
        if Y == 2:
            add(n, rows(index(c, 1 - y, 0), Z), r_core[n, rows((1 - y) * Z, Z), :])
            side_copy(n).start()
        add(n, rows(index(c, y, 0), Z), r_core[n, rows(y * Z, Z), :])

    def after_side(n):
        if Y == 2:
            side_copy(n).wait_recv()
            add(n, rows(index(c, y, 0), Z), r_side[n])

    def along(n, way):
        source = has_down if way == UP else has_up
        for step in range(Z - 1):
            goal = Z - 1 - step if way == UP else step

            def move(goal=goal):
                @pl.when(source)
                def _():
                    line_copy(n, goal, way).wait_recv()
                    slot = goal + 1 if way == UP else goal
                    add(n, rows(index(c, y, goal)), r_line[n, rows(slot), :])

                line_copy(n, goal, way).start()

            pl.when(goal > z if way == UP else goal < z)(move)

    def complete(n):
        at = pl.ds(n * width, width)
        fin[...] = part[n, rows(own), :].astype(jnp.float32)

        @pl.when(has_down)
        def _():
            line_copy(n, z, UP).wait_recv()
            fin[...] += r_line[n, rows(z + 1), :].astype(jnp.float32)

        @pl.when(has_up)
        def _():
            line_copy(n, z, DOWN).wait_recv()
            fin[...] += r_line[n, rows(z), :].astype(jnp.float32)

        fin[...] += stream_ref[:, at].astype(jnp.float32)
        drafts = out_ref.shape[1]
        for r in range(out_ref.shape[0]):
            out_ref[r, :, at] = fin[r * drafts : (r + 1) * drafts, :].astype(jnp.bfloat16)

    if C == 1:
        produce(0)
        after_core(0)
        after_side(0)
        along(0, UP)
        along(0, DOWN)
        complete(0)
    else:
        for t in range(C + Z + 4):
            if t < C:
                produce(t)
            if 0 <= t - 1 < C:
                after_core(t - 1)
            if 0 <= t - 2 < C:
                after_side(t - 2)
            for hop in range(Z - 1):
                n = t - 2 - hop
                if 0 <= n < C:
                    pl.when(z == hop)(functools.partial(along, n, UP))
                    pl.when(z == Z - 1 - hop)(functools.partial(along, n, DOWN))
            if 0 <= t - 2 - Z < C:
                complete(t - 2 - Z)

    for k in range(C):
        for d in range(Z):
            line_step(d, k, finish)
            if Y == 2:
                side_step(d, k, finish)
        core_copy(k).wait_send()
        if Y == 2:
            side_copy(k).wait_send()
        for goal in range(Z):
            pl.when(goal > z)(lambda goal=goal: line_copy(k, goal, UP).wait_send())
            pl.when(goal < z)(lambda goal=goal: line_copy(k, goal, DOWN).wait_send())


def feed(C, Z, Y, shape, normed, stream, wg, wu, wd):
    R, D = stream.shape
    ff = wg.shape[1]
    N = 2 * Y * Z
    M = N * R
    width = D // C
    bf16 = jnp.bfloat16
    dma = pltpu.SemaphoreType.DMA
    vmem = pl.BlockSpec(memory_space=pltpu.VMEM)
    hbm = pl.BlockSpec(memory_space=pl.ANY)
    return pl.pallas_call(
        functools.partial(feed_kernel, C, Z, Y),
        out_shape=jax.ShapeDtypeStruct(shape, bf16),
        in_specs=[vmem, vmem, hbm, hbm, hbm],
        out_specs=vmem,
        scratch_shapes=[
            pltpu.VMEM((C, M, width), bf16),
            pltpu.VMEM((D, ff), bf16),
            pltpu.VMEM((D, ff), bf16),
            pltpu.VMEM((ff, D), bf16),
            pltpu.VMEM((M, ff), jnp.float32),
            pltpu.VMEM((M, ff), jnp.float32),
            pltpu.VMEM((M, ff), bf16),
            pltpu.VMEM((C, M, width), bf16),
            pltpu.VMEM((C, M // 2, width), bf16),
            pltpu.VMEM((C, Z * R, width), bf16),
            pltpu.VMEM((C, (Z + 1) * R, width), bf16),
            pltpu.VMEM((R, width), jnp.float32),
            dma((3, C)),
            dma((4, C, N)),
            dma((C, N)),
            dma((C,)),
            dma((C,)),
            dma((C,)),
            dma((C,)),
            dma((C, Z)),
            dma((C, Z + 1)),
        ],
        compiler_params=pltpu.CompilerParams(
            collective_id=0, has_side_effects=True, vmem_limit_bytes=58 * 1024 * 1024
        ),
        cost_estimate=pl.CostEstimate(
            flops=6 * M * D * ff, bytes_accessed=6 * D * ff, transcendentals=M * ff
        ),
    )(normed, stream, wg, wu, wd)


def shards(
    Z,
    Y,
    C,
    queries,
    new_keys,
    new_values,
    key_cache,
    value_cache,
    residual_in,
    norm_gain,
    gate_weight,
    up_weight,
    down_weight,
    live_counts,
    cache_lengths,
    positions,
):
    requests = residual_in.shape[0]
    stream, normed = attend(
        C, queries, new_keys, new_values, key_cache, value_cache,
        residual_in, norm_gain,
        cache_lengths, positions,
    )
    combined = feed(C, Z, Y, residual_in.shape, normed, stream, gate_weight, up_weight, down_weight)
    live_slot = jnp.arange(requests) < live_counts[0]
    return jnp.where(live_slot[:, None, None], combined, jnp.zeros_like(combined))


def solution(mesh):
    ffn = mesh.shape["ffn"]
    Y = 2 if ffn % 2 == 0 and ffn <= 8 else 1
    C = 4 if ffn <= 8 else 1
    return jax.shard_map(
        functools.partial(shards, ffn // Y, Y, C),
        mesh=mesh,
        in_specs=(
            P(("rep", "attn", "ffn"), None, None),
            P(("rep", "attn", "ffn"), None, None),
            P(("rep", "attn", "ffn"), None, None),
            P(("rep", "attn", "ffn"), None, None),
            P(("rep", "attn", "ffn"), None, None),
            P(("rep", "attn", "ffn"), None, None),
            P(),
            P(None, ("attn", "ffn")),
            P(None, ("attn", "ffn")),
            P(("attn", "ffn"), None),
            P(("rep", "attn", "ffn")),
            P(("rep", "attn", "ffn")),
            P(("rep", "attn", "ffn")),
        ),
        out_specs=P(("rep", "attn", "ffn"), None, None),
        check_vma=False,
    )
```

```python
import functools

import jax
import jax.numpy as jnp
from jax import lax
from jax.experimental import pallas as pl
from jax.experimental.pallas import tpu as pltpu
from jax.sharding import PartitionSpec as P

HEADS = 32
KVH = 4
HD = 128


rope_base = 500000.0
norm_epsilon = 1e-05

MESH = pl.DeviceIdType.MESH
UP, DOWN, SIDE, CORE = range(4)


def attention_rows(
    inputs, lengths_ref, cos_ref, sin_ref, batch, arrived, hidden_start,
    stream_ref, write_normed, C, wide_ref, heads_ref, mixed_ref,
):
    q_ref, dk_ref, dv_ref, residual_ref, gain_ref, k_ref, v_ref = inputs
    slots = k_ref.shape[1]
    requests = q_ref.shape[0]
    count = 2 * requests
    group = HEADS // KVH
    scale = HD ** (-0.5)
    rows = 2 * HEADS

    def widen(ref):
        for r in range(requests):
            wide_ref[2 * r : 2 * r + 2, :] = ref[r].astype(jnp.float32)

    def rotate(value, cosine, sine):
        return value * cosine + pltpu.roll(value, HD // 2, 1) * sine

    for i in range(5):
        arrived[i].wait()
    widen(q_ref)
    for h in range(HEADS):
        value = rotate(wide_ref[:, h * HD : (h + 1) * HD], cos_ref[...], sin_ref[...])
        heads_ref[pl.ds(h, count, stride=HEADS), :] = value
    widen(residual_ref)

    late = (lax.broadcasted_iota(jnp.int32, (rows, 1), 0) // group) % 2 == 1
    column = lax.broadcasted_iota(jnp.int32, (rows, slots), 1)

    def spread(part, t):
        return jnp.concatenate(
            [
                jnp.broadcast_to(part[t : t + 1, g * HD : (g + 1) * HD], (2 * group, HD))
                for g in range(KVH)
            ],
            axis=0,
        )

    for step in range(requests // batch):
        arrived[5 + 2 * step].wait()
        arrived[6 + 2 * step].wait()
        if step == requests // batch - 1:
            hidden_start()
        picked = []
        for b in range(batch):
            r = step * batch + b
            first_row = r * rows
            q = jnp.concatenate(
                [
                    heads_ref[pl.ds(first_row + s * HEADS + g * group, group), :]
                    for g in range(KVH)
                    for s in range(2)
                ],
                axis=0,
            ).astype(jnp.bfloat16)
            scores = jnp.concatenate(
                [
                    lax.dot_general(
                        q[g * 2 * group : (g + 1) * 2 * group],
                        k_ref[r, :, g * HD : (g + 1) * HD],
                        (((1,), (1,)), ((), ())),
                        preferred_element_type=jnp.float32,
                    )
                    for g in range(KVH)
                ],
                axis=0,
            ) * scale
            scores = jnp.where(column < lengths_ref[r], scores, -jnp.inf)
            cosine, sine = cos_ref[pl.ds(2 * r, 2), :], sin_ref[pl.ds(2 * r, 2), :]
            fresh = dk_ref[r].astype(jnp.float32)
            fresh = jnp.concatenate(
                [rotate(fresh[:, g * HD : (g + 1) * HD], cosine, sine) for g in range(KVH)], axis=1
            ).astype(jnp.bfloat16).astype(jnp.float32)
            wide = q.astype(jnp.float32)
            first = jnp.sum(wide * spread(fresh, 0), axis=-1, keepdims=True) * scale
            second = jnp.sum(wide * spread(fresh, 1), axis=-1, keepdims=True) * scale
            second = jnp.where(late, second, -jnp.inf)
            picked.append((r, scores, first, second))

        for b in range(batch):
            r, scores, first, second = picked[b]
            highest = jnp.maximum(jnp.max(scores, axis=-1, keepdims=True), jnp.maximum(first, second))
            scores = jnp.exp(scores - highest)
            first = jnp.exp(first - highest)
            second = jnp.exp(second - highest)
            total = 1.0 / (jnp.sum(scores, axis=-1, keepdims=True) + first + second)
            weights = (scores * total).astype(jnp.bfloat16)
            first = (first * total).astype(jnp.bfloat16).astype(jnp.float32)
            second = (second * total).astype(jnp.bfloat16).astype(jnp.float32)
            fresh = dv_ref[r].astype(jnp.float32)
            extra = first * spread(fresh, 0) + second * spread(fresh, 1)
            first_row = r * rows
            for g in range(KVH):
                at = slice(g * 2 * group, (g + 1) * 2 * group)
                mixed = extra[at] + jnp.dot(
                    weights[at], v_ref[r, :, g * HD : (g + 1) * HD], preferred_element_type=jnp.float32
                )
                for s in range(2):
                    mixed_ref[pl.ds(first_row + s * HEADS + g * group, group), :] = mixed[
                        s * group : (s + 1) * group
                    ]

    square = jnp.zeros((count, HD), jnp.float32)
    for h in range(HEADS):
        at = slice(h * HD, (h + 1) * HD)
        value = wide_ref[:, at] + mixed_ref[pl.ds(h, count, stride=HEADS), :]
        value = value.astype(jnp.bfloat16)
        stream_ref[:, at] = value
        value = value.astype(jnp.float32)
        square += value * value
    mean = jnp.sum(square, axis=-1, keepdims=True) / (HEADS * HD)
    factor = lax.rsqrt(mean + norm_epsilon)
    width = HEADS * HD // C
    for k in range(C):
        at = slice(k * width, (k + 1) * width)
        write_normed(k, (
            stream_ref[:, at].astype(jnp.float32) * factor * gain_ref[at].astype(jnp.float32)[None, :]
        ).astype(jnp.bfloat16))


def turn_tables(requests, drafts, positions):
    place = jnp.arange(HD)
    frequency = rope_base ** (-2.0 * (place % (HD // 2)).astype(jnp.float32) / HD)
    row = jnp.arange(requests * drafts)
    offsets = jnp.repeat(positions, drafts).astype(jnp.float32) + (row % drafts).astype(jnp.float32)
    angles = offsets[:, None] * frequency[None, :]
    sine = jnp.sin(angles)
    return jnp.cos(angles), jnp.where(place[None, :] < HD // 2, -sine, sine)


def feed_kernel(
    C, Z, Y, lengths_ref, cos_ref, sin_ref, q_hbm, dk_hbm, dv_hbm, residual_hbm, gain_hbm,
    k_hbm, v_hbm, wg_hbm, wu_hbm, wd_hbm, out_ref,
    q_in, dk_in, dv_in, residual_in, gain_in, k_in, v_in, stream_ref, wide, heads, mixed, in_sem,
    gath, wg, wu, wd, acc_g, acc_u, hid, part, r_core, r_side, r_line, fin,
    w_sem, ag_send, ag_recv, core_send, core_recv, side_send, side_recv, line_send, line_recv,
):
    c = lax.axis_index("attn")
    f = lax.axis_index("ffn")
    z, y = f // Y, f % Y
    R = stream_ref.shape[0]
    N = 2 * Y * Z
    kc = gath.shape[2]
    width = part.shape[2]
    up = {"ffn": (z + 1) * Y + y}
    down = {"ffn": (z - 1) * Y + y}
    side = {"ffn": z * Y + (Y - 1 - y)}
    core = {"attn": 1 - c}
    targets = [up, down, side, core]
    has_up, has_down = z < Z - 1, z > 0

    requests = q_in.shape[0]
    batch = 4 if requests % 4 == 0 else 1
    arrived = []
    fetched = ((q_hbm, q_in), (dk_hbm, dk_in), (dv_hbm, dv_in), (residual_hbm, residual_in), (gain_hbm, gain_in))
    for source, place in fetched:
        arrived.append(pltpu.make_async_copy(source, place, in_sem.at[len(arrived)]))
    for step in range(requests // batch):
        at = pl.ds(step * batch, batch)
        for source, place in ((k_hbm, k_in), (v_hbm, v_in)):
            arrived.append(pltpu.make_async_copy(source.at[at], place.at[at], in_sem.at[len(arrived)]))
    for copy in arrived:
        copy.start()

    weight_copies = []
    for k in range(C):
        at = pl.ds(k * kc, kc)
        weight_copies.append(pltpu.make_async_copy(wg_hbm.at[at, :], wg.at[at, :], w_sem.at[0, k]))
        weight_copies.append(pltpu.make_async_copy(wu_hbm.at[at, :], wu.at[at, :], w_sem.at[1, k]))
    for n in range(C):
        at = pl.ds(n * width, width)
        weight_copies.append(pltpu.make_async_copy(wd_hbm.at[:, at], wd.at[:, at], w_sem.at[2, n]))

    def weights_start():
        for copy in weight_copies:
            copy.start()

    barrier = pltpu.get_barrier_semaphore()

    def greet(target):
        pl.semaphore_signal(barrier, inc=1, device_id=target, device_id_type=MESH)

    greet(core)
    if Y == 2:
        greet(side)
    pl.when(has_up)(lambda: greet(up))
    pl.when(has_down)(lambda: greet(down))

    def index(cc, yy, zz):
        return (cc * Y + yy) * Z + zz

    def rows(at, count=1):
        return pl.ds(pl.multiple_of(at * R, R), count * R)

    own = index(c, y, z)

    def write_normed(k, value):
        gath[k, rows(own), :] = value

    attention_rows(
        (q_in, dk_in, dv_in, residual_in, gain_in, k_in, v_in), lengths_ref, cos_ref, sin_ref,
        batch, arrived, weights_start, stream_ref, write_normed, C, wide, heads, mixed,
    )

    peers = 2 if Y == 2 else 1
    ends = jnp.logical_or(z == 0, z == Z - 1)
    pl.when(ends)(lambda: pl.semaphore_wait(barrier, peers + 1))
    pl.when(jnp.logical_not(ends))(lambda: pl.semaphore_wait(barrier, peers + 2))

    def ag(k, block, way):
        at = gath.at[k, rows(block), :]
        return pltpu.make_async_remote_copy(
            src_ref=at, dst_ref=at, send_sem=ag_send.at[way, k, block],
            recv_sem=ag_recv.at[k, block], device_id=targets[way], device_id_type=MESH,
        )

    def line_step(d, k, act):
        if d == 0:
            pl.when(has_up)(lambda: act(k, own, UP))
            pl.when(has_down)(lambda: act(k, own, DOWN))
            if Y == 2:
                act(k, own, SIDE)
            act(k, own, CORE)
            return

        def arrived(block, way, more):
            if act is start:
                ag(k, block, way).wait_recv()
            pl.when(more)(lambda: act(k, block, way))
            if Y == 2:
                act(k, block, SIDE)
            act(k, block, CORE)

        pl.when(z - d >= 0)(lambda: arrived(index(c, y, z - d), UP, has_up))
        pl.when(z + d < Z)(lambda: arrived(index(c, y, z + d), DOWN, has_down))

    def side_step(d, k, act):
        def arrived(block):
            if act is start:
                ag(k, block, SIDE).wait_recv()
            act(k, block, CORE)

        if d == 0:
            arrived(index(c, 1 - y, z))
        else:
            pl.when(z - d >= 0)(lambda: arrived(index(c, 1 - y, z - d)))
            pl.when(z + d < Z)(lambda: arrived(index(c, 1 - y, z + d)))

    def start(k, block, way):
        ag(k, block, way).start()

    def finish(k, block, way):
        ag(k, block, way).wait_send()

    def project(k):
        for j in range(Y * Z):
            ag(k, (1 - c) * Y * Z + j, CORE).wait_recv()
        weight_copies[2 * k].wait()
        weight_copies[2 * k + 1].wait()
        at = pl.ds(k * kc, kc)
        ff = wg.shape[1]
        x = gath[k]
        if ff % 128 == 0:
            both = jnp.concatenate([wg[at, :], wu[at, :]], axis=1)
            both = jnp.dot(x, both, preferred_element_type=jnp.float32)
            new_g, new_u = both[:, :ff], both[:, ff:]
        else:
            new_g = jnp.dot(x, wg[at, :], preferred_element_type=jnp.float32)
            new_u = jnp.dot(x, wu[at, :], preferred_element_type=jnp.float32)
        if k > 0:
            new_g = acc_g[...] + new_g
            new_u = acc_u[...] + new_u
        if k < C - 1:
            acc_g[...] = new_g
            acc_u[...] = new_u
        else:
            hid[...] = (new_g / (1.0 + jnp.exp(-new_g)) * new_u).astype(jnp.bfloat16)

    lag = 2
    for t in range(C + Z + lag):
        for d in range(Z):
            if 0 <= t - d < C:
                line_step(d, t - d, start)
        if Y == 2:
            for d in range(Z):
                if 0 <= t - lag - d < C:
                    side_step(d, t - lag - d, start)
        k = t - lag - (Z - 1)
        if 0 <= k < C:
            project(k)

    half = Y * Z

    def core_copy(n):
        return pltpu.make_async_remote_copy(
            src_ref=part.at[n, rows((1 - c) * half, half), :], dst_ref=r_core.at[n],
            send_sem=core_send.at[n], recv_sem=core_recv.at[n],
            device_id=core, device_id_type=MESH,
        )

    def side_copy(n):
        return pltpu.make_async_remote_copy(
            src_ref=part.at[n, rows(index(c, 1 - y, 0), Z), :], dst_ref=r_side.at[n],
            send_sem=side_send.at[n], recv_sem=side_recv.at[n],
            device_id=side, device_id_type=MESH,
        )

    def line_copy(n, goal, way):
        slot = goal + 1 if way == UP else goal
        return pltpu.make_async_remote_copy(
            src_ref=part.at[n, rows(index(c, y, goal)), :], dst_ref=r_line.at[n, rows(slot), :],
            send_sem=line_send.at[n, goal], recv_sem=line_recv.at[n, slot],
            device_id=targets[way], device_id_type=MESH,
        )

    def add(n, at, other):
        part[n, at, :] = (
            part[n, at, :].astype(jnp.float32) + other.astype(jnp.float32)
        ).astype(jnp.bfloat16)

    def produce(n):
        weight_copies[2 * C + n].wait()
        at = pl.ds(n * width, width)
        part[n] = jnp.dot(
            hid[...], wd[:, at], preferred_element_type=jnp.float32
        ).astype(jnp.bfloat16)
        core_copy(n).start()

    def after_core(n):
        core_copy(n).wait_recv()
        if Y == 2:
            add(n, rows(index(c, 1 - y, 0), Z), r_core[n, rows((1 - y) * Z, Z), :])
            side_copy(n).start()
        add(n, rows(index(c, y, 0), Z), r_core[n, rows(y * Z, Z), :])

    def after_side(n):
        if Y == 2:
            side_copy(n).wait_recv()
            add(n, rows(index(c, y, 0), Z), r_side[n])

    def along(n, way):
        source = has_down if way == UP else has_up
        for step in range(Z - 1):
            goal = Z - 1 - step if way == UP else step

            def move(goal=goal):
                @pl.when(source)
                def _():
                    line_copy(n, goal, way).wait_recv()
                    slot = goal + 1 if way == UP else goal
                    add(n, rows(index(c, y, goal)), r_line[n, rows(slot), :])

                line_copy(n, goal, way).start()

            pl.when(goal > z if way == UP else goal < z)(move)

    def complete(n):
        at = pl.ds(n * width, width)
        fin[...] = part[n, rows(own), :].astype(jnp.float32)

        @pl.when(has_down)
        def _():
            line_copy(n, z, UP).wait_recv()
            fin[...] += r_line[n, rows(z + 1), :].astype(jnp.float32)

        @pl.when(has_up)
        def _():
            line_copy(n, z, DOWN).wait_recv()
            fin[...] += r_line[n, rows(z), :].astype(jnp.float32)

        fin[...] += stream_ref[:, at].astype(jnp.float32)
        drafts = out_ref.shape[1]
        for r in range(out_ref.shape[0]):
            out_ref[r, :, at] = fin[r * drafts : (r + 1) * drafts, :].astype(jnp.bfloat16)

    if C == 1:
        produce(0)
        after_core(0)
        after_side(0)
        along(0, UP)
        along(0, DOWN)
        complete(0)
    else:
        for t in range(C + Z + 4):
            if t < C:
                produce(t)
            if 0 <= t - 1 < C:
                after_core(t - 1)
            if 0 <= t - 2 < C:
                after_side(t - 2)
            for hop in range(Z - 1):
                n = t - 2 - hop
                if 0 <= n < C:
                    pl.when(z == hop)(functools.partial(along, n, UP))
                    pl.when(z == Z - 1 - hop)(functools.partial(along, n, DOWN))
            if 0 <= t - 2 - Z < C:
                complete(t - 2 - Z)

    for k in range(C):
        for d in range(Z):
            line_step(d, k, finish)
            if Y == 2:
                side_step(d, k, finish)
        core_copy(k).wait_send()
        if Y == 2:
            side_copy(k).wait_send()
        for goal in range(Z):
            pl.when(goal > z)(lambda goal=goal: line_copy(k, goal, UP).wait_send())
            pl.when(goal < z)(lambda goal=goal: line_copy(k, goal, DOWN).wait_send())


def layer(C, Z, Y, lengths, cosine, sine, *arrays):
    queries, new_keys, new_values, residual, gain, key_cache, value_cache, wg, wu, wd = arrays
    shape = residual.shape
    requests, drafts, D = shape
    R = requests * drafts
    ff = wg.shape[1]
    N = 2 * Y * Z
    M = N * R
    width = D // C
    bf16 = jnp.bfloat16
    dma = pltpu.SemaphoreType.DMA
    vmem = pl.BlockSpec(memory_space=pltpu.VMEM)
    hbm = pl.BlockSpec(memory_space=pl.ANY)
    return pl.pallas_call(
        functools.partial(feed_kernel, C, Z, Y),
        out_shape=jax.ShapeDtypeStruct(shape, bf16),
        in_specs=[pl.BlockSpec(memory_space=pltpu.SMEM), vmem, vmem] + [hbm] * 10,
        out_specs=vmem,
        scratch_shapes=[pltpu.VMEM(array.shape, bf16) for array in arrays[:7]] + [
            pltpu.VMEM((R, D), bf16),
            pltpu.VMEM((R, D), jnp.float32),
            pltpu.VMEM((R * HEADS, HD), jnp.float32),
            pltpu.VMEM((R * HEADS, HD), jnp.float32),
            dma((5 + 2 * requests,)),
            pltpu.VMEM((C, M, width), bf16),
            pltpu.VMEM((D, ff), bf16),
            pltpu.VMEM((D, ff), bf16),
            pltpu.VMEM((ff, D), bf16),
            pltpu.VMEM((M, ff), jnp.float32),
            pltpu.VMEM((M, ff), jnp.float32),
            pltpu.VMEM((M, ff), bf16),
            pltpu.VMEM((C, M, width), bf16),
            pltpu.VMEM((C, M // 2, width), bf16),
            pltpu.VMEM((C, Z * R, width), bf16),
            pltpu.VMEM((C, (Z + 1) * R, width), bf16),
            pltpu.VMEM((R, width), jnp.float32),
            dma((3, C)),
            dma((4, C, N)),
            dma((C, N)),
            dma((C,)),
            dma((C,)),
            dma((C,)),
            dma((C,)),
            dma((C, Z)),
            dma((C, Z + 1)),
        ],
        compiler_params=pltpu.CompilerParams(
            collective_id=0, has_side_effects=True, vmem_limit_bytes=58 * 1024 * 1024
        ),
        cost_estimate=pl.CostEstimate(
            flops=6 * M * D * ff, bytes_accessed=6 * D * ff, transcendentals=M * ff
        ),
    )(lengths, cosine, sine, *arrays)


def shards(
    Z,
    Y,
    C,
    queries,
    new_keys,
    new_values,
    key_cache,
    value_cache,
    residual_in,
    norm_gain,
    gate_weight,
    up_weight,
    down_weight,
    live_counts,
    cache_lengths,
    positions,
):
    requests = residual_in.shape[0]
    cosine, sine = turn_tables(requests, residual_in.shape[1], positions)
    combined = layer(
        C, Z, Y, cache_lengths, cosine, sine, queries, new_keys, new_values, residual_in, norm_gain,
        key_cache, value_cache, gate_weight, up_weight, down_weight,
    )
    live_slot = jnp.arange(requests) < live_counts[0]
    return jnp.where(live_slot[:, None, None], combined, jnp.zeros_like(combined))


def solution(mesh):
    ffn = mesh.shape["ffn"]
    Y = 2 if ffn % 2 == 0 and ffn <= 8 else 1
    C = 4 if ffn <= 8 else 1
    return jax.shard_map(
        functools.partial(shards, ffn // Y, Y, C),
        mesh=mesh,
        in_specs=(
            P(("rep", "attn", "ffn"), None, None),
            P(("rep", "attn", "ffn"), None, None),
            P(("rep", "attn", "ffn"), None, None),
            P(("rep", "attn", "ffn"), None, None),
            P(("rep", "attn", "ffn"), None, None),
            P(("rep", "attn", "ffn"), None, None),
            P(),
            P(None, ("attn", "ffn")),
            P(None, ("attn", "ffn")),
            P(("attn", "ffn"), None),
            P(("rep", "attn", "ffn")),
            P(("rep", "attn", "ffn")),
            P(("rep", "attn", "ffn")),
        ),
        out_specs=P(("rep", "attn", "ffn"), None, None),
        check_vma=False,
    )
```

```python
import functools

import jax
import jax.numpy as jnp
from jax import lax
from jax.experimental import pallas as pl
from jax.experimental.pallas import tpu as pltpu
from jax.sharding import PartitionSpec as P

HEADS = 32
KVH = 4
HD = 128


rope_base = 500000.0
norm_epsilon = 1e-05

MESH = pl.DeviceIdType.MESH
SIDE, CORE = range(2)


def attention_rows(
    inputs, lengths_ref, cos_ref, sin_ref, batch, arrived, hidden_start,
    stream_ref, write_normed, C, wide_ref, heads_ref, mixed_ref,
):
    q_ref, dk_ref, dv_ref, residual_ref, gain_ref, k_ref, v_ref = inputs
    slots = k_ref.shape[1]
    requests = q_ref.shape[0]
    count = 2 * requests
    group = HEADS // KVH
    scale = HD ** (-0.5)
    rows = 2 * HEADS

    def widen(ref):
        for r in range(requests):
            wide_ref[2 * r : 2 * r + 2, :] = ref[r].astype(jnp.float32)

    def rotate(value, cosine, sine):
        return value * cosine + pltpu.roll(value, HD // 2, 1) * sine

    for i in range(5):
        arrived[i].wait()
    widen(q_ref)
    for h in range(HEADS):
        value = rotate(wide_ref[:, h * HD : (h + 1) * HD], cos_ref[...], sin_ref[...])
        heads_ref[pl.ds(h, count, stride=HEADS), :] = value
    widen(residual_ref)

    late = (lax.broadcasted_iota(jnp.int32, (rows, 1), 0) // group) % 2 == 1
    column = lax.broadcasted_iota(jnp.int32, (rows, slots), 1)

    def spread(part, t):
        return jnp.concatenate(
            [
                jnp.broadcast_to(part[t : t + 1, g * HD : (g + 1) * HD], (2 * group, HD))
                for g in range(KVH)
            ],
            axis=0,
        )

    for step in range(requests // batch):
        arrived[5 + 2 * step].wait()
        arrived[6 + 2 * step].wait()
        if step == requests // batch - 1:
            hidden_start()
        picked = []
        for b in range(batch):
            r = step * batch + b
            first_row = r * rows
            q = jnp.concatenate(
                [
                    heads_ref[pl.ds(first_row + s * HEADS + g * group, group), :]
                    for g in range(KVH)
                    for s in range(2)
                ],
                axis=0,
            ).astype(jnp.bfloat16)
            scores = jnp.concatenate(
                [
                    lax.dot_general(
                        q[g * 2 * group : (g + 1) * 2 * group],
                        k_ref[r, :, g * HD : (g + 1) * HD],
                        (((1,), (1,)), ((), ())),
                        preferred_element_type=jnp.float32,
                    )
                    for g in range(KVH)
                ],
                axis=0,
            ) * scale
            scores = jnp.where(column < lengths_ref[r], scores, -jnp.inf)
            cosine, sine = cos_ref[pl.ds(2 * r, 2), :], sin_ref[pl.ds(2 * r, 2), :]
            fresh = dk_ref[r].astype(jnp.float32)
            fresh = jnp.concatenate(
                [rotate(fresh[:, g * HD : (g + 1) * HD], cosine, sine) for g in range(KVH)], axis=1
            ).astype(jnp.bfloat16).astype(jnp.float32)
            wide = q.astype(jnp.float32)
            first = jnp.sum(wide * spread(fresh, 0), axis=-1, keepdims=True) * scale
            second = jnp.sum(wide * spread(fresh, 1), axis=-1, keepdims=True) * scale
            second = jnp.where(late, second, -jnp.inf)
            picked.append((r, scores, first, second))

        for b in range(batch):
            r, scores, first, second = picked[b]
            highest = jnp.maximum(jnp.max(scores, axis=-1, keepdims=True), jnp.maximum(first, second))
            scores = jnp.exp(scores - highest)
            first = jnp.exp(first - highest)
            second = jnp.exp(second - highest)
            total = 1.0 / (jnp.sum(scores, axis=-1, keepdims=True) + first + second)
            weights = (scores * total).astype(jnp.bfloat16)
            first = (first * total).astype(jnp.bfloat16).astype(jnp.float32)
            second = (second * total).astype(jnp.bfloat16).astype(jnp.float32)
            fresh = dv_ref[r].astype(jnp.float32)
            extra = first * spread(fresh, 0) + second * spread(fresh, 1)
            first_row = r * rows
            for g in range(KVH):
                at = slice(g * 2 * group, (g + 1) * 2 * group)
                mixed = extra[at] + jnp.dot(
                    weights[at], v_ref[r, :, g * HD : (g + 1) * HD], preferred_element_type=jnp.float32
                )
                for s in range(2):
                    mixed_ref[pl.ds(first_row + s * HEADS + g * group, group), :] = mixed[
                        s * group : (s + 1) * group
                    ]

    square = jnp.zeros((count, HD), jnp.float32)
    for h in range(HEADS):
        at = slice(h * HD, (h + 1) * HD)
        value = wide_ref[:, at] + mixed_ref[pl.ds(h, count, stride=HEADS), :]
        value = value.astype(jnp.bfloat16)
        stream_ref[:, at] = value
        value = value.astype(jnp.float32)
        square += value * value
    mean = jnp.sum(square, axis=-1, keepdims=True) / (HEADS * HD)
    factor = lax.rsqrt(mean + norm_epsilon)
    width = HEADS * HD // C
    for k in range(C):
        at = slice(k * width, (k + 1) * width)
        write_normed(k, (
            stream_ref[:, at].astype(jnp.float32) * factor * gain_ref[at].astype(jnp.float32)[None, :]
        ).astype(jnp.bfloat16))


def turn_tables(requests, drafts, positions):
    place = jnp.arange(HD)
    frequency = rope_base ** (-2.0 * (place % (HD // 2)).astype(jnp.float32) / HD)
    row = jnp.arange(requests * drafts)
    offsets = jnp.repeat(positions, drafts).astype(jnp.float32) + (row % drafts).astype(jnp.float32)
    angles = offsets[:, None] * frequency[None, :]
    sine = jnp.sin(angles)
    return jnp.cos(angles), jnp.where(place[None, :] < HD // 2, -sine, sine)


def feed_kernel(
    C, Z, Y, lengths_ref, cos_ref, sin_ref, q_hbm, dk_hbm, dv_hbm, residual_hbm, gain_hbm,
    k_hbm, v_hbm, wg_hbm, wu_hbm, wd_hbm, out_ref,
    q_in, dk_in, dv_in, residual_in, gain_in, k_in, v_in, stream_ref, wide, heads, mixed, in_sem,
    gath, wg, wu, wd, acc_g, acc_u, hid, part, r_core, r_side, r_line, fin,
    w_sem, out_send, ag_send, ag_recv, core_send, core_recv, side_send, side_recv, line_send, line_recv,
):
    c = lax.axis_index("attn")
    f = lax.axis_index("ffn")
    z, y = f // Y, f % Y
    R = stream_ref.shape[0]
    N = 2 * Y * Z
    kc = gath.shape[2]
    width = part.shape[2]
    side = {"ffn": z * Y + (Y - 1 - y)}
    core = {"attn": 1 - c}
    targets = [side, core]

    def ahead(d):
        return lax.rem(z + d, Z)

    def behind(d):
        return lax.rem(z + Z - d, Z)

    requests = q_in.shape[0]
    batch = 4 if requests % 4 == 0 else 1
    arrived = []
    fetched = ((q_hbm, q_in), (dk_hbm, dk_in), (dv_hbm, dv_in), (residual_hbm, residual_in), (gain_hbm, gain_in))
    for source, place in fetched:
        arrived.append(pltpu.make_async_copy(source, place, in_sem.at[len(arrived)]))
    for step in range(requests // batch):
        at = pl.ds(step * batch, batch)
        for source, place in ((k_hbm, k_in), (v_hbm, v_in)):
            arrived.append(pltpu.make_async_copy(source.at[at], place.at[at], in_sem.at[len(arrived)]))
    for copy in arrived:
        copy.start()

    weight_copies = []
    for k in range(C):
        at = pl.ds(k * kc, kc)
        weight_copies.append(pltpu.make_async_copy(wg_hbm.at[at, :], wg.at[at, :], w_sem.at[0, k]))
        weight_copies.append(pltpu.make_async_copy(wu_hbm.at[at, :], wu.at[at, :], w_sem.at[1, k]))
    for n in range(C):
        at = pl.ds(n * width, width)
        weight_copies.append(pltpu.make_async_copy(wd_hbm.at[:, at], wd.at[:, at], w_sem.at[2, n]))

    def weights_start():
        for copy in weight_copies:
            copy.start()

    barrier = pltpu.get_barrier_semaphore()

    def greet(target):
        pl.semaphore_signal(barrier, inc=1, device_id=target, device_id_type=MESH)

    greet(core)
    if Y == 2:
        greet(side)
    for d in range(1, Z):
        greet({"ffn": ahead(d) * Y + y})

    def index(cc, yy, zz):
        return (cc * Y + yy) * Z + zz

    def rows(at, count=1):
        return pl.ds(pl.multiple_of(at * R, R), count * R)

    own = index(c, y, z)

    def write_normed(k, value):
        gath[k, rows(own), :] = value

    attention_rows(
        (q_in, dk_in, dv_in, residual_in, gain_in, k_in, v_in), lengths_ref, cos_ref, sin_ref,
        batch, arrived, weights_start, stream_ref, write_normed, C, wide, heads, mixed,
    )

    pl.semaphore_wait(barrier, (Z - 1) + Y)

    def line_out(k, d):
        at = gath.at[k, rows(own), :]
        return pltpu.make_async_remote_copy(
            src_ref=at, dst_ref=at, send_sem=out_send.at[k, d], recv_sem=ag_recv.at[k, own],
            device_id={"ffn": ahead(d) * Y + y}, device_id_type=MESH,
        )

    def ag(k, block, way):
        at = gath.at[k, rows(block), :]
        return pltpu.make_async_remote_copy(
            src_ref=at, dst_ref=at, send_sem=ag_send.at[way, k, block],
            recv_sem=ag_recv.at[k, block], device_id=targets[way], device_id_type=MESH,
        )

    def line_step(d, k, act):
        block = own if d == 0 else index(c, y, behind(d))
        if d == 0:
            for e in range(1, Z):
                if act is start:
                    line_out(k, e).start()
                else:
                    line_out(k, e).wait_send()
        elif act is start:
            ag(k, block, CORE).wait_recv()
        if Y == 2:
            act(k, block, SIDE)
        act(k, block, CORE)

    def side_step(d, k, act):
        block = index(c, 1 - y, behind(d))
        if act is start:
            ag(k, block, SIDE).wait_recv()
        act(k, block, CORE)

    def start(k, block, way):
        ag(k, block, way).start()

    def finish(k, block, way):
        ag(k, block, way).wait_send()

    def project(k):
        for j in range(Y * Z):
            ag(k, (1 - c) * Y * Z + j, CORE).wait_recv()
        weight_copies[2 * k].wait()
        weight_copies[2 * k + 1].wait()
        at = pl.ds(k * kc, kc)
        ff = wg.shape[1]
        x = gath[k]
        if ff % 128 == 0:
            both = jnp.concatenate([wg[at, :], wu[at, :]], axis=1)
            both = jnp.dot(x, both, preferred_element_type=jnp.float32)
            new_g, new_u = both[:, :ff], both[:, ff:]
        else:
            new_g = jnp.dot(x, wg[at, :], preferred_element_type=jnp.float32)
            new_u = jnp.dot(x, wu[at, :], preferred_element_type=jnp.float32)
        if k > 0:
            new_g = acc_g[...] + new_g
            new_u = acc_u[...] + new_u
        if k < C - 1:
            acc_g[...] = new_g
            acc_u[...] = new_u
        else:
            hid[...] = (new_g / (1.0 + jnp.exp(-new_g)) * new_u).astype(jnp.bfloat16)

    for k in range(C):
        line_step(0, k, start)
    for k in range(C + 2):
        for d in range(1, Z):
            if k < C:
                line_step(d, k, start)
        for d in range(Z):
            if Y == 2 and 0 <= k - 1 < C:
                side_step(d, k - 1, start)
        if k >= 2:
            project(k - 2)

    half = Y * Z

    def core_copy(n):
        return pltpu.make_async_remote_copy(
            src_ref=part.at[n, rows((1 - c) * half, half), :], dst_ref=r_core.at[n],
            send_sem=core_send.at[n], recv_sem=core_recv.at[n],
            device_id=core, device_id_type=MESH,
        )

    def side_copy(n):
        return pltpu.make_async_remote_copy(
            src_ref=part.at[n, rows(index(c, 1 - y, 0), Z), :], dst_ref=r_side.at[n],
            send_sem=side_send.at[n], recv_sem=side_recv.at[n],
            device_id=side, device_id_type=MESH,
        )

    def line_copy(n, d):
        return pltpu.make_async_remote_copy(
            src_ref=part.at[n, rows(index(c, y, ahead(d))), :], dst_ref=r_line.at[n, rows(d), :],
            send_sem=line_send.at[n, d], recv_sem=line_recv.at[n, d],
            device_id={"ffn": ahead(d) * Y + y}, device_id_type=MESH,
        )

    def add(n, at, other):
        part[n, at, :] = (
            part[n, at, :].astype(jnp.float32) + other.astype(jnp.float32)
        ).astype(jnp.bfloat16)

    def produce(n):
        weight_copies[2 * C + n].wait()
        at = pl.ds(n * width, width)
        part[n] = jnp.dot(
            hid[...], wd[:, at], preferred_element_type=jnp.float32
        ).astype(jnp.bfloat16)
        core_copy(n).start()

    def after_core(n):
        core_copy(n).wait_recv()
        if Y == 2:
            add(n, rows(index(c, 1 - y, 0), Z), r_core[n, rows((1 - y) * Z, Z), :])
            side_copy(n).start()
        add(n, rows(index(c, y, 0), Z), r_core[n, rows(y * Z, Z), :])

    def after_side(n):
        if Y == 2:
            side_copy(n).wait_recv()
            add(n, rows(index(c, y, 0), Z), r_side[n])

    def along(n):
        for d in range(1, Z):
            line_copy(n, d).start()

    def complete(n):
        at = pl.ds(n * width, width)
        fin[...] = part[n, rows(own), :].astype(jnp.float32)

        for d in range(1, Z):
            line_copy(n, d).wait_recv()
            fin[...] += r_line[n, rows(d), :].astype(jnp.float32)

        fin[...] += stream_ref[:, at].astype(jnp.float32)
        drafts = out_ref.shape[1]
        for r in range(out_ref.shape[0]):
            out_ref[r, :, at] = fin[r * drafts : (r + 1) * drafts, :].astype(jnp.bfloat16)

    for t in range(C + 4):
        if t < C:
            produce(t)
        if 0 <= t - 1 < C:
            after_core(t - 1)
        if 0 <= t - 2 < C:
            after_side(t - 2)
            along(t - 2)
        if 0 <= t - 4 < C:
            complete(t - 4)

    for k in range(C):
        for d in range(Z):
            line_step(d, k, finish)
            if Y == 2:
                side_step(d, k, finish)
        core_copy(k).wait_send()
        if Y == 2:
            side_copy(k).wait_send()
        for d in range(1, Z):
            line_copy(k, d).wait_send()


def layer(C, Z, Y, lengths, cosine, sine, *arrays):
    queries, new_keys, new_values, residual, gain, key_cache, value_cache, wg, wu, wd = arrays
    shape = residual.shape
    requests, drafts, D = shape
    R = requests * drafts
    ff = wg.shape[1]
    N = 2 * Y * Z
    M = N * R
    width = D // C
    bf16 = jnp.bfloat16
    dma = pltpu.SemaphoreType.DMA
    vmem = pl.BlockSpec(memory_space=pltpu.VMEM)
    hbm = pl.BlockSpec(memory_space=pl.ANY)
    return pl.pallas_call(
        functools.partial(feed_kernel, C, Z, Y),
        out_shape=jax.ShapeDtypeStruct(shape, bf16),
        in_specs=[pl.BlockSpec(memory_space=pltpu.SMEM), vmem, vmem] + [hbm] * 10,
        out_specs=vmem,
        scratch_shapes=[pltpu.VMEM(array.shape, bf16) for array in arrays[:7]] + [
            pltpu.VMEM((R, D), bf16),
            pltpu.VMEM((R, D), jnp.float32),
            pltpu.VMEM((R * HEADS, HD), jnp.float32),
            pltpu.VMEM((R * HEADS, HD), jnp.float32),
            dma((5 + 2 * requests,)),
            pltpu.VMEM((C, M, width), bf16),
            pltpu.VMEM((D, ff), bf16),
            pltpu.VMEM((D, ff), bf16),
            pltpu.VMEM((ff, D), bf16),
            pltpu.VMEM((M, ff), jnp.float32),
            pltpu.VMEM((M, ff), jnp.float32),
            pltpu.VMEM((M, ff), bf16),
            pltpu.VMEM((C, M, width), bf16),
            pltpu.VMEM((C, M // 2, width), bf16),
            pltpu.VMEM((C, Z * R, width), bf16),
            pltpu.VMEM((C, (Z + 1) * R, width), bf16),
            pltpu.VMEM((R, width), jnp.float32),
            dma((3, C)),
            dma((C, Z)),
            dma((2, C, N)),
            dma((C, N)),
            dma((C,)),
            dma((C,)),
            dma((C,)),
            dma((C,)),
            dma((C, Z)),
            dma((C, Z + 1)),
        ],
        compiler_params=pltpu.CompilerParams(
            collective_id=0, has_side_effects=True, vmem_limit_bytes=58 * 1024 * 1024
        ),
        cost_estimate=pl.CostEstimate(
            flops=6 * M * D * ff, bytes_accessed=6 * D * ff, transcendentals=M * ff
        ),
    )(lengths, cosine, sine, *arrays)


def shards(
    Z,
    Y,
    C,
    queries,
    new_keys,
    new_values,
    key_cache,
    value_cache,
    residual_in,
    norm_gain,
    gate_weight,
    up_weight,
    down_weight,
    live_counts,
    cache_lengths,
    positions,
):
    requests = residual_in.shape[0]
    cosine, sine = turn_tables(requests, residual_in.shape[1], positions)
    combined = layer(
        C, Z, Y, cache_lengths, cosine, sine, queries, new_keys, new_values, residual_in, norm_gain,
        key_cache, value_cache, gate_weight, up_weight, down_weight,
    )
    live_slot = jnp.arange(requests) < live_counts[0]
    return jnp.where(live_slot[:, None, None], combined, jnp.zeros_like(combined))


def solution(mesh):
    ffn = mesh.shape["ffn"]
    Y = 2 if ffn % 2 == 0 and ffn <= 8 else 1
    C = 4 if ffn <= 8 else 1
    return jax.shard_map(
        functools.partial(shards, ffn // Y, Y, C),
        mesh=mesh,
        in_specs=(
            P(("rep", "attn", "ffn"), None, None),
            P(("rep", "attn", "ffn"), None, None),
            P(("rep", "attn", "ffn"), None, None),
            P(("rep", "attn", "ffn"), None, None),
            P(("rep", "attn", "ffn"), None, None),
            P(("rep", "attn", "ffn"), None, None),
            P(),
            P(None, ("attn", "ffn")),
            P(None, ("attn", "ffn")),
            P(("attn", "ffn"), None),
            P(("rep", "attn", "ffn")),
            P(("rep", "attn", "ffn")),
            P(("rep", "attn", "ffn")),
        ),
        out_specs=P(("rep", "attn", "ffn"), None, None),
        check_vma=False,
    )
```

```python
import functools

import jax
import jax.numpy as jnp
from jax import lax
from jax.experimental import pallas as pl
from jax.experimental.pallas import tpu as pltpu
from jax.sharding import PartitionSpec as P

HEADS = 32
KVH = 4
HD = 128


rope_base = 500000.0
norm_epsilon = 1e-05

MESH = pl.DeviceIdType.MESH
SIDE, CORE = range(2)


def attention_rows(
    inputs, lengths_ref, cos_ref, sin_ref, batch, arrived, hidden_start,
    stream_ref, write_normed, C, wide_ref, heads_ref, mixed_ref,
):
    q_ref, dk_ref, dv_ref, residual_ref, gain_ref, k_ref, v_ref = inputs
    slots = k_ref.shape[1]
    requests = q_ref.shape[0]
    count = 2 * requests
    group = HEADS // KVH
    scale = HD ** (-0.5)
    rows = 2 * HEADS

    def widen(ref):
        for r in range(requests):
            wide_ref[2 * r : 2 * r + 2, :] = ref[r].astype(jnp.float32)

    def rotate(value, cosine, sine):
        return value * cosine + pltpu.roll(value, HD // 2, 1) * sine

    for i in range(5):
        arrived[i].wait()
    widen(q_ref)
    for h in range(HEADS):
        value = rotate(wide_ref[:, h * HD : (h + 1) * HD], cos_ref[...], sin_ref[...])
        heads_ref[pl.ds(h, count, stride=HEADS), :] = value
    widen(residual_ref)

    late = (lax.broadcasted_iota(jnp.int32, (rows, 1), 0) // group) % 2 == 1
    column = lax.broadcasted_iota(jnp.int32, (rows, slots), 1)

    def spread(part, t):
        return jnp.concatenate(
            [
                jnp.broadcast_to(part[t : t + 1, g * HD : (g + 1) * HD], (2 * group, HD))
                for g in range(KVH)
            ],
            axis=0,
        )

    for step in range(requests // batch):
        arrived[5 + 2 * step].wait()
        arrived[6 + 2 * step].wait()
        if step == requests // batch - 1:
            hidden_start()
        picked = []
        for b in range(batch):
            r = step * batch + b
            first_row = r * rows
            q = jnp.concatenate(
                [
                    heads_ref[pl.ds(first_row + s * HEADS + g * group, group), :]
                    for g in range(KVH)
                    for s in range(2)
                ],
                axis=0,
            ).astype(jnp.bfloat16)
            scores = jnp.concatenate(
                [
                    lax.dot_general(
                        q[g * 2 * group : (g + 1) * 2 * group],
                        k_ref[r, :, g * HD : (g + 1) * HD],
                        (((1,), (1,)), ((), ())),
                        preferred_element_type=jnp.float32,
                    )
                    for g in range(KVH)
                ],
                axis=0,
            ) * scale
            scores = jnp.where(column < lengths_ref[r], scores, -jnp.inf)
            cosine, sine = cos_ref[pl.ds(2 * r, 2), :], sin_ref[pl.ds(2 * r, 2), :]
            fresh = dk_ref[r].astype(jnp.float32)
            fresh = jnp.concatenate(
                [rotate(fresh[:, g * HD : (g + 1) * HD], cosine, sine) for g in range(KVH)], axis=1
            ).astype(jnp.bfloat16).astype(jnp.float32)
            wide = q.astype(jnp.float32)
            first = jnp.sum(wide * spread(fresh, 0), axis=-1, keepdims=True) * scale
            second = jnp.sum(wide * spread(fresh, 1), axis=-1, keepdims=True) * scale
            second = jnp.where(late, second, -jnp.inf)
            picked.append((r, scores, first, second))

        for b in range(batch):
            r, scores, first, second = picked[b]
            highest = jnp.maximum(jnp.max(scores, axis=-1, keepdims=True), jnp.maximum(first, second))
            scores = jnp.exp(scores - highest)
            first = jnp.exp(first - highest)
            second = jnp.exp(second - highest)
            total = 1.0 / (jnp.sum(scores, axis=-1, keepdims=True) + first + second)
            weights = (scores * total).astype(jnp.bfloat16)
            first = (first * total).astype(jnp.bfloat16).astype(jnp.float32)
            second = (second * total).astype(jnp.bfloat16).astype(jnp.float32)
            fresh = dv_ref[r].astype(jnp.float32)
            extra = first * spread(fresh, 0) + second * spread(fresh, 1)
            first_row = r * rows
            for g in range(KVH):
                at = slice(g * 2 * group, (g + 1) * 2 * group)
                mixed = extra[at] + jnp.dot(
                    weights[at], v_ref[r, :, g * HD : (g + 1) * HD], preferred_element_type=jnp.float32
                )
                for s in range(2):
                    mixed_ref[pl.ds(first_row + s * HEADS + g * group, group), :] = mixed[
                        s * group : (s + 1) * group
                    ]

    square = jnp.zeros((count, HD), jnp.float32)
    for h in range(HEADS):
        at = slice(h * HD, (h + 1) * HD)
        value = wide_ref[:, at] + mixed_ref[pl.ds(h, count, stride=HEADS), :]
        value = value.astype(jnp.bfloat16)
        stream_ref[:, at] = value
        value = value.astype(jnp.float32)
        square += value * value
    mean = jnp.sum(square, axis=-1, keepdims=True) / (HEADS * HD)
    factor = lax.rsqrt(mean + norm_epsilon)
    width = HEADS * HD // C
    for k in range(C):
        at = slice(k * width, (k + 1) * width)
        write_normed(k, (
            stream_ref[:, at].astype(jnp.float32) * factor * gain_ref[at].astype(jnp.float32)[None, :]
        ).astype(jnp.bfloat16))


def turn_tables(requests, drafts, positions):
    place = jnp.arange(HD)
    frequency = rope_base ** (-2.0 * (place % (HD // 2)).astype(jnp.float32) / HD)
    row = jnp.arange(requests * drafts)
    offsets = jnp.repeat(positions, drafts).astype(jnp.float32) + (row % drafts).astype(jnp.float32)
    angles = offsets[:, None] * frequency[None, :]
    sine = jnp.sin(angles)
    return jnp.cos(angles), jnp.where(place[None, :] < HD // 2, -sine, sine)


def feed_kernel(
    C, Z, Y, live_ref, lengths_ref, cos_ref, sin_ref, q_hbm, dk_hbm, dv_hbm, residual_hbm, gain_hbm,
    k_hbm, v_hbm, wg_hbm, wu_hbm, wd_hbm, out_ref,
    q_in, dk_in, dv_in, residual_in, gain_in, k_in, v_in, stream_ref, wide, heads, mixed, in_sem,
    gath, wg, wu, wd, acc_g, acc_u, hid, part, r_core, r_side, r_line, fin,
    w_sem, out_send, ag_send, ag_recv, core_send, core_recv, side_send, side_recv, line_send, line_recv,
):
    c = lax.axis_index("attn")
    f = lax.axis_index("ffn")
    z, y = f // Y, f % Y
    R = stream_ref.shape[0]
    N = 2 * Y * Z
    kc = gath.shape[2]
    width = part.shape[2]
    side = {"ffn": z * Y + (Y - 1 - y)}
    core = {"attn": 1 - c}
    targets = [side, core]

    def ahead(d):
        return lax.rem(z + d, Z)

    def behind(d):
        return lax.rem(z + Z - d, Z)

    requests = q_in.shape[0]
    batch = 4 if requests % 4 == 0 else 1
    arrived = []
    fetched = ((q_hbm, q_in), (dk_hbm, dk_in), (dv_hbm, dv_in), (residual_hbm, residual_in), (gain_hbm, gain_in))
    for source, place in fetched:
        arrived.append(pltpu.make_async_copy(source, place, in_sem.at[len(arrived)]))
    for step in range(requests // batch):
        at = pl.ds(step * batch, batch)
        for source, place in ((k_hbm, k_in), (v_hbm, v_in)):
            arrived.append(pltpu.make_async_copy(source.at[at], place.at[at], in_sem.at[len(arrived)]))
    for copy in arrived:
        copy.start()

    weight_copies = []
    for k in range(C):
        at = pl.ds(k * kc, kc)
        weight_copies.append(pltpu.make_async_copy(wg_hbm.at[at, :], wg.at[at, :], w_sem.at[0, k]))
        weight_copies.append(pltpu.make_async_copy(wu_hbm.at[at, :], wu.at[at, :], w_sem.at[1, k]))
    for n in range(C):
        at = pl.ds(n * width, width)
        weight_copies.append(pltpu.make_async_copy(wd_hbm.at[:, at], wd.at[:, at], w_sem.at[2, n]))

    def weights_start():
        for copy in weight_copies:
            copy.start()

    barrier = pltpu.get_barrier_semaphore()

    def greet(target):
        pl.semaphore_signal(barrier, inc=1, device_id=target, device_id_type=MESH)

    greet(core)
    if Y == 2:
        greet(side)
    for d in range(1, Z):
        greet({"ffn": ahead(d) * Y + y})

    def index(cc, yy, zz):
        return (cc * Y + yy) * Z + zz

    def rows(at, count=1):
        return pl.ds(pl.multiple_of(at * R, R), count * R)

    own = index(c, y, z)

    def write_normed(k, value):
        gath[k, rows(own), :] = value

    attention_rows(
        (q_in, dk_in, dv_in, residual_in, gain_in, k_in, v_in), lengths_ref, cos_ref, sin_ref,
        batch, arrived, weights_start, stream_ref, write_normed, C, wide, heads, mixed,
    )

    pl.semaphore_wait(barrier, (Z - 1) + Y)

    def line_out(k, d):
        at = gath.at[k, rows(own), :]
        return pltpu.make_async_remote_copy(
            src_ref=at, dst_ref=at, send_sem=out_send.at[k, d], recv_sem=ag_recv.at[k, own],
            device_id={"ffn": ahead(d) * Y + y}, device_id_type=MESH,
        )

    def ag(k, block, way):
        at = gath.at[k, rows(block), :]
        return pltpu.make_async_remote_copy(
            src_ref=at, dst_ref=at, send_sem=ag_send.at[way, k, block],
            recv_sem=ag_recv.at[k, block], device_id=targets[way], device_id_type=MESH,
        )

    def line_step(d, k, act):
        block = own if d == 0 else index(c, y, behind(d))
        if d == 0:
            for e in range(1, Z):
                if act is start:
                    line_out(k, e).start()
                else:
                    line_out(k, e).wait_send()
        elif act is start:
            ag(k, block, CORE).wait_recv()
        if Y == 2:
            act(k, block, SIDE)
        act(k, block, CORE)

    def side_step(d, k, act):
        block = index(c, 1 - y, behind(d))
        if act is start:
            ag(k, block, SIDE).wait_recv()
        act(k, block, CORE)

    def start(k, block, way):
        ag(k, block, way).start()

    def finish(k, block, way):
        ag(k, block, way).wait_send()

    def project(k):
        for j in range(Y * Z):
            ag(k, (1 - c) * Y * Z + j, CORE).wait_recv()
        weight_copies[2 * k].wait()
        weight_copies[2 * k + 1].wait()
        at = pl.ds(k * kc, kc)
        ff = wg.shape[1]
        x = gath[k]
        if ff % 128 == 0:
            both = jnp.concatenate([wg[at, :], wu[at, :]], axis=1)
            both = jnp.dot(x, both, preferred_element_type=jnp.float32)
            new_g, new_u = both[:, :ff], both[:, ff:]
        else:
            new_g = jnp.dot(x, wg[at, :], preferred_element_type=jnp.float32)
            new_u = jnp.dot(x, wu[at, :], preferred_element_type=jnp.float32)
        if k > 0:
            new_g = acc_g[...] + new_g
            new_u = acc_u[...] + new_u
        if k < C - 1:
            acc_g[...] = new_g
            acc_u[...] = new_u
        else:
            hid[...] = (new_g / (1.0 + jnp.exp(-new_g)) * new_u).astype(jnp.bfloat16)

    for k in range(C):
        line_step(0, k, start)
    for k in range(C + 2):
        for d in range(1, Z):
            if k < C:
                line_step(d, k, start)
        for d in range(Z):
            if Y == 2 and 0 <= k - 1 < C:
                side_step(d, k - 1, start)
        if k >= 2:
            project(k - 2)

    half = Y * Z

    def core_copy(n):
        return pltpu.make_async_remote_copy(
            src_ref=part.at[n, rows((1 - c) * half, half), :], dst_ref=r_core.at[n],
            send_sem=core_send.at[n], recv_sem=core_recv.at[n],
            device_id=core, device_id_type=MESH,
        )

    def side_copy(n):
        return pltpu.make_async_remote_copy(
            src_ref=part.at[n, rows(index(c, 1 - y, 0), Z), :], dst_ref=r_side.at[n],
            send_sem=side_send.at[n], recv_sem=side_recv.at[n],
            device_id=side, device_id_type=MESH,
        )

    def line_copy(n, d):
        return pltpu.make_async_remote_copy(
            src_ref=part.at[n, rows(index(c, y, ahead(d))), :], dst_ref=r_line.at[n, rows(d), :],
            send_sem=line_send.at[n, d], recv_sem=line_recv.at[n, d],
            device_id={"ffn": ahead(d) * Y + y}, device_id_type=MESH,
        )

    def add(n, at, other):
        part[n, at, :] = (
            part[n, at, :].astype(jnp.float32) + other.astype(jnp.float32)
        ).astype(jnp.bfloat16)

    def produce(n):
        weight_copies[2 * C + n].wait()
        at = pl.ds(n * width, width)
        part[n] = jnp.dot(
            hid[...], wd[:, at], preferred_element_type=jnp.float32
        ).astype(jnp.bfloat16)
        core_copy(n).start()

    def after_core(n):
        core_copy(n).wait_recv()
        if Y == 2:
            add(n, rows(index(c, 1 - y, 0), Z), r_core[n, rows((1 - y) * Z, Z), :])
            side_copy(n).start()
        add(n, rows(index(c, y, 0), Z), r_core[n, rows(y * Z, Z), :])

    def after_side(n):
        if Y == 2:
            side_copy(n).wait_recv()
            add(n, rows(index(c, y, 0), Z), r_side[n])

    def along(n):
        for d in range(1, Z):
            line_copy(n, d).start()

    def complete(n):
        at = pl.ds(n * width, width)
        fin[...] = part[n, rows(own), :].astype(jnp.float32)

        for d in range(1, Z):
            line_copy(n, d).wait_recv()
            fin[...] += r_line[n, rows(d), :].astype(jnp.float32)

        drafts = out_ref.shape[1]
        live = lax.broadcasted_iota(jnp.int32, fin.shape, 0) < live_ref[0] * drafts
        fin[...] = jnp.where(live, fin[...] + stream_ref[:, at].astype(jnp.float32), 0.0)
        for r in range(out_ref.shape[0]):
            out_ref[r, :, at] = fin[r * drafts : (r + 1) * drafts, :].astype(jnp.bfloat16)

    for t in range(C + 4):
        if t < C:
            produce(t)
        if 0 <= t - 1 < C:
            after_core(t - 1)
        if 0 <= t - 2 < C:
            after_side(t - 2)
            along(t - 2)
        if 0 <= t - 4 < C:
            complete(t - 4)

    for k in range(C):
        for d in range(Z):
            line_step(d, k, finish)
            if Y == 2:
                side_step(d, k, finish)
        core_copy(k).wait_send()
        if Y == 2:
            side_copy(k).wait_send()
        for d in range(1, Z):
            line_copy(k, d).wait_send()


def layer(C, Z, Y, live, lengths, cosine, sine, *arrays):
    queries, new_keys, new_values, residual, gain, key_cache, value_cache, wg, wu, wd = arrays
    shape = residual.shape
    requests, drafts, D = shape
    R = requests * drafts
    ff = wg.shape[1]
    N = 2 * Y * Z
    M = N * R
    width = D // C
    bf16 = jnp.bfloat16
    dma = pltpu.SemaphoreType.DMA
    vmem = pl.BlockSpec(memory_space=pltpu.VMEM)
    hbm = pl.BlockSpec(memory_space=pl.ANY)
    return pl.pallas_call(
        functools.partial(feed_kernel, C, Z, Y),
        out_shape=jax.ShapeDtypeStruct(shape, bf16),
        in_specs=[pl.BlockSpec(memory_space=pltpu.SMEM)] * 2 + [vmem, vmem] + [hbm] * 10,
        out_specs=vmem,
        scratch_shapes=[pltpu.VMEM(array.shape, bf16) for array in arrays[:7]] + [
            pltpu.VMEM((R, D), bf16),
            pltpu.VMEM((R, D), jnp.float32),
            pltpu.VMEM((R * HEADS, HD), jnp.float32),
            pltpu.VMEM((R * HEADS, HD), jnp.float32),
            dma((5 + 2 * requests,)),
            pltpu.VMEM((C, M, width), bf16),
            pltpu.VMEM((D, ff), bf16),
            pltpu.VMEM((D, ff), bf16),
            pltpu.VMEM((ff, D), bf16),
            pltpu.VMEM((M, ff), jnp.float32),
            pltpu.VMEM((M, ff), jnp.float32),
            pltpu.VMEM((M, ff), bf16),
            pltpu.VMEM((C, M, width), bf16),
            pltpu.VMEM((C, M // 2, width), bf16),
            pltpu.VMEM((C, Z * R, width), bf16),
            pltpu.VMEM((C, (Z + 1) * R, width), bf16),
            pltpu.VMEM((R, width), jnp.float32),
            dma((3, C)),
            dma((C, Z)),
            dma((2, C, N)),
            dma((C, N)),
            dma((C,)),
            dma((C,)),
            dma((C,)),
            dma((C,)),
            dma((C, Z)),
            dma((C, Z + 1)),
        ],
        compiler_params=pltpu.CompilerParams(
            collective_id=0, has_side_effects=True, vmem_limit_bytes=58 * 1024 * 1024
        ),
        cost_estimate=pl.CostEstimate(
            flops=6 * M * D * ff, bytes_accessed=6 * D * ff, transcendentals=M * ff
        ),
    )(live, lengths, cosine, sine, *arrays)


def shards(
    Z,
    Y,
    C,
    queries,
    new_keys,
    new_values,
    key_cache,
    value_cache,
    residual_in,
    norm_gain,
    gate_weight,
    up_weight,
    down_weight,
    live_counts,
    cache_lengths,
    positions,
):
    requests = residual_in.shape[0]
    cosine, sine = turn_tables(requests, residual_in.shape[1], positions)
    return layer(
        C, Z, Y, live_counts, cache_lengths, cosine, sine, queries, new_keys, new_values, residual_in, norm_gain,
        key_cache, value_cache, gate_weight, up_weight, down_weight,
    )


def solution(mesh):
    ffn = mesh.shape["ffn"]
    Y = 2 if ffn % 2 == 0 and ffn <= 8 else 1
    C = 4 if ffn <= 8 else 1
    return jax.shard_map(
        functools.partial(shards, ffn // Y, Y, C),
        mesh=mesh,
        in_specs=(
            P(("rep", "attn", "ffn"), None, None),
            P(("rep", "attn", "ffn"), None, None),
            P(("rep", "attn", "ffn"), None, None),
            P(("rep", "attn", "ffn"), None, None),
            P(("rep", "attn", "ffn"), None, None),
            P(("rep", "attn", "ffn"), None, None),
            P(),
            P(None, ("attn", "ffn")),
            P(None, ("attn", "ffn")),
            P(("attn", "ffn"), None),
            P(("rep", "attn", "ffn")),
            P(("rep", "attn", "ffn")),
            P(("rep", "attn", "ffn")),
        ),
        out_specs=P(("rep", "attn", "ffn"), None, None),
        check_vma=False,
    )
```
